32 devices in a mesh: row: 8 (over z, y), col: 4 (over x, core).
Axes of the slice: x: 2, y: 2, z: 4, core: 2. Of those that a mesh axis runs over, the one named last changes fastest.
Arguments:
- right_side: bfloat16 [256, 32, 128], P(('row', 'col')), may hold values from -6 to 6
- leaf_lower: bfloat16 [256, 128, 128], P(('row', 'col')), may hold values from -0.5 to 0.5
- leaf_upper: bfloat16 [256, 128, 128], P(('row', 'col')), may hold values from -0.5 to 0.5
- lower_blocks: bfloat16 [256, 2, 128, 1024], P(('row', 'col')), may hold values from -0.09375 to 0.09375
- upper_blocks: bfloat16 [256, 2, 1024, 128], P(('row', 'col')), may hold values from -0.125 to 0.125
- parent_rhs: bfloat16 [16, 32, 1024], P('row'), may hold values from -6 to 6
- parent_lower: bfloat16 [16, 1024, 1024], P('row', None, 'col'), may hold values from -0.1875 to 0.1875
- parent_upper: bfloat16 [16, 1024, 1024], P('row', None, 'col'), may hold values from -0.1875 to 0.1875
- targets: int32 [256, 2], P(('row', 'col')), may hold values from 0 to 3, all different within a row
Outputs:
- leaf_solution: float32 [256, 32, 128], P(('row', 'col'))
- parent_solution: float32 [16, 32, 1024], P('row', None, 'col')
The draws below stay inside these ranges and needn't reach their ends.
Inputs may be any that keep to these rules, and one draw needn't show every extreme that they name: `targets`: each leaf lists 2 different window indices; index j below 2 names a parent of the leaf's own process row, the others one of the next row (the last row's next is the first).
All inputs are finite; a program needn't handle non-finite values.
Results may differ from the reference program's by a relative error of at most 0.0075.
Values may be sent and summed in bfloat16 or wider, within the bound.
No kernel may reach another device: no remote copies, remote signals or barrier semaphores. Data moves between devices by JAX's collectives and lax.ppermute only.
A program may use at most 128 MiB of HBM per device.

```python
import jax
import jax.numpy as jnp
from jax import lax

W = 128
WB = 1024
NRHS = 32
K = 2
A_DEV = 8
B_DEV = 2
NA = 256
NB = 16
N_ROW = 8
N_COL = 4


def levels(own_key, extent, shards, low, largest):
    level, own = 1.0, jax.random.fold_in(own_key, 6)
    for dim, blocks in shards:
        draws = jnp.exp(jax.random.uniform(jax.random.fold_in(own, dim), (blocks,), jnp.float32, low / len(shards), largest / len(shards)))
        level = level * jnp.repeat(draws, extent[dim] // blocks).reshape([-1 if axis == dim else 1 for axis in range(len(extent))])
    return level


def choose_distinct(key, rows, number_of, top, lift):
    sequence = jax.random.permutation(jax.random.fold_in(key, 1), number_of)
    favour = sequence
    for power in range(3):
        favour = favour * favour // number_of
    favour = favour * lift // number_of
    tickets = jax.random.randint(jax.random.fold_in(key, 2), (rows, number_of), 0, 4096) + favour
    holders = jax.random.permutation(jax.random.fold_in(key, 3), rows)[jnp.arange(number_of) % rows]
    tickets = jnp.where(jnp.arange(rows)[:, None] == holders[None, :], 1 << 14, tickets)
    priority = tickets * number_of + jnp.arange(number_of)
    return lax.top_k(priority.astype(jnp.int32), top)[1].astype(jnp.int32)


def gaussian(stream_key, dims, spread, reach, split=(), held_as=jnp.bfloat16):
    values = spread * jax.random.normal(stream_key, dims, jnp.float32)
    if split:
        values = values * levels(stream_key, dims, split, -0.22, 0.18)
    return jnp.clip(values, -reach, reach).astype(held_as)


def setup_inputs(seed: int = 0) -> dict:
    seeds = jax.random.split(jax.random.key(seed), 10)
    right_side = gaussian(seeds[0], (NA, NRHS, W), 1.0, 6.0, ((0, 32),))
    leaf_lower = gaussian(seeds[1], (NA, W, W), W ** -0.5, 0.5, ((0, 32),))
    leaf_upper = gaussian(seeds[2], (NA, W, W), W ** -0.5, 0.5, ((0, 32),))
    lower_blocks = gaussian(seeds[3], (NA, K, W, WB), (W * N_COL * A_DEV * K // B_DEV) ** -0.5, 0.09375, ((0, 32),))
    upper_blocks = gaussian(seeds[4], (NA, K, WB, W), (K * WB) ** -0.5, 0.125, ((0, 32),))
    parent_rhs = gaussian(seeds[5], (NB, NRHS, WB), 1.0, 6.0, ((0, 8),))
    parent_lower = gaussian(seeds[6], (NB, WB, WB), WB ** -0.5, 0.1875, ((0, 8), (2, 4)))
    parent_upper = gaussian(seeds[7], (NB, WB, WB), WB ** -0.5, 0.1875, ((0, 8), (2, 4)))
    targets = choose_distinct(seeds[8], NA, 2 * B_DEV, K, 8192)
    return {"right_side": right_side, "leaf_lower": leaf_lower, "leaf_upper": leaf_upper, "lower_blocks": lower_blocks, "upper_blocks": upper_blocks, "parent_rhs": parent_rhs, "parent_lower": parent_lower, "parent_upper": parent_upper, "targets": targets}


def widen(value):
    return value.astype(jnp.float32)


def parent_ids(device, window):
    row_index = device // N_COL
    return ((row_index + window // B_DEV) % N_ROW) * B_DEV + window % B_DEV


def reference(right_side, leaf_lower, leaf_upper, lower_blocks, upper_blocks, parent_rhs, parent_lower, parent_upper, targets):
    highest = lax.Precision.HIGHEST
    count = N_ROW * N_COL

    def blockwise(value):
        return value.reshape((count, A_DEV) + value.shape[1:])

    devices = jnp.arange(count, dtype=jnp.int32)

    def forward_step(update, items):
        device, rhs_block, lower_inv, blocks, listed = items
        solved = jnp.einsum('anw,awv->anv', widen(rhs_block), widen(lower_inv), precision=highest).astype(jnp.bfloat16)
        terms = jnp.einsum('anw,akwv->aknv', widen(solved), widen(blocks), precision=highest)
        owners = parent_ids(device, listed).reshape(-1).astype(jnp.int32)
        update = update.at[owners].add(terms.reshape(A_DEV * K, NRHS, WB))
        return update, solved

    start = jnp.zeros((NB, NRHS, WB), jnp.float32)
    update, solved = lax.scan(forward_step, start, (devices, blockwise(right_side), blockwise(leaf_lower), blockwise(lower_blocks), blockwise(targets)))
    combined = (widen(parent_rhs) - update).astype(jnp.bfloat16)
    forward_parent = jnp.einsum('tnw,twv->tnv', widen(combined), widen(parent_lower), precision=highest).astype(jnp.bfloat16)
    parent_solution = jnp.einsum('tnw,twv->tnv', widen(forward_parent), widen(parent_upper), precision=highest)
    rounded = parent_solution.astype(jnp.bfloat16)

    def backward_step(carry, items):
        device, solved_block, blocks, upper_inv, listed = items
        owners = parent_ids(device, listed).astype(jnp.int32)
        picked = rounded[owners]
        coupling = jnp.einsum('aknv,akvw->anw', widen(picked), widen(blocks), precision=highest)
        reduced = (widen(solved_block) - coupling).astype(jnp.bfloat16)
        result = jnp.einsum('anw,awv->anv', widen(reduced), widen(upper_inv), precision=highest)
        return carry, result

    unused, leaf_parts = lax.scan(backward_step, jnp.zeros((), jnp.float32), (devices, solved, blockwise(upper_blocks), blockwise(leaf_upper), blockwise(targets)))
    leaf_solution = leaf_parts.reshape(NA, NRHS, W)
    return leaf_solution, parent_solution
```

```python
import functools

import jax
import jax.numpy as jnp
from jax import lax
from jax.experimental import pallas as pl
from jax.experimental.pallas import tpu as pltpu
from jax.sharding import PartitionSpec as P

CORES = 2
F32 = jnp.float32
BF16 = jnp.bfloat16
VMEM = pl.BlockSpec(memory_space=pltpu.VMEM)
SMEM = pl.BlockSpec(memory_space=pltpu.SMEM)
ANY = pl.BlockSpec(memory_space=pl.ANY)


def dot(a, b):
    return jnp.dot(a, b, preferred_element_type=F32)


def send(array, rows, cols, by_row, by_chip, flip):
    chips = cols // CORES
    pairs = []
    for row in range(rows):
        for col in range(cols):
            chip, core = col // CORES, col % CORES
            to = ((chip + by_chip) % chips) * CORES + (core ^ flip)
            pairs.append((row * cols + col, ((row + by_row) % rows) * cols + to))
    return lax.ppermute(array, ("row", "col"), pairs)


def forward_kernel(where, targets, rhs_hbm, lower_hbm, blocks_hbm, solved_ref, keep_ref, send_ref, rhs, lower, blocks, acc, sems):
    leaves, k, width, wide = blocks.shape
    nrhs = rhs.shape[1]
    first = [
        pltpu.make_async_copy(rhs_hbm, rhs, sems.at[0]),
        pltpu.make_async_copy(lower_hbm, lower, sems.at[1]),
    ]
    copies = [pltpu.make_async_copy(blocks_hbm.at[a], blocks.at[a], sems.at[2 + a]) for a in range(leaves)]
    for copy in first + copies:
        copy.start()
    core = where[0]
    slots = (core, 2 + core, 1 - core, 3 - core)
    for copy in first:
        copy.wait()
    solved = [dot(rhs[a], lower[a]).astype(BF16) for a in range(leaves)]
    for a in range(leaves):
        solved_ref[a] = solved[a]
    step = 2
    for a0 in range(0, leaves, step):
        for a in range(a0, a0 + step):
            copies[a].wait()
        lhs = jnp.concatenate(
            [
                jnp.concatenate(
                    [
                        jnp.where(targets[a, i] == slot, solved[a], jnp.zeros_like(solved[a]))
                        for a in range(a0, a0 + step)
                        for i in range(k)
                    ],
                    axis=1,
                )
                for slot in slots
            ],
            axis=0,
        )
        part = dot(lhs, blocks[pl.ds(a0, step)].reshape(step * k * width, wide))
        if a0 == 0:
            acc[...] = part
        elif a0 + step < leaves:
            acc[...] += part
        else:
            total = acc[...] + part
            keep_ref[...] = total[: 2 * nrhs].reshape(2, nrhs, wide)
            send_ref[...] = total[2 * nrhs :].astype(BF16).reshape(2, nrhs, wide)


def parent_kernel(pieces, incoming, where, keep, came, rhs, lower, lower_other, upper, *rest):
    rest = list(rest)
    others = [rest.pop(0) for _ in range(pieces)]
    sums = [rest.pop(0) for _ in range(incoming)]
    full_ref, half_ref, forward = rest
    core, chip = where[0], where[1]
    chips = pieces + 1
    chips = (pieces + 1) // CORES
    cut = lower.shape[2]
    update = keep[0] + came[0].astype(F32)
    for term in sums:
        update = update + term[...].astype(F32)
    combined = (rhs[core].astype(F32) - update).astype(BF16)
    mine = pl.multiple_of(core * cut, cut)
    theirs = pl.multiple_of((1 - core) * cut, cut)
    forward[:, pl.ds(mine, cut)] = dot(combined, lower[core]).astype(BF16)
    forward[:, pl.ds(theirs, cut)] = dot(combined, lower_other[...]).astype(BF16)
    depth = forward.shape[1]
    lhs = forward[...]
    rows = pl.ds(pl.multiple_of(chip * depth, depth), depth)
    piece = 0
    for by in range(chips):
        for flip in range(CORES):
            source = lax.rem(chip + chips - by, chips) * CORES + (core if flip == 0 else 1 - core)
            if by == 0 and flip == 0:
                block = upper[core, rows, :]
            else:
                block = others[piece][...]
                piece += 1
            part = dot(lhs, block)
            at = pl.ds(pl.multiple_of(source * cut, cut), cut)
            full_ref[:, at] = part
            half_ref[:, at] = part.astype(BF16)


def backward_kernel(where, targets, solved, own, mine, theirs, blocks_hbm, upper, leaf_ref, parent_ref, window, blocks, sems):
    leaves, k, wide, width = blocks.shape
    copies = [pltpu.make_async_copy(blocks_hbm.at[a], blocks.at[a], sems.at[a]) for a in range(leaves)]
    for copy in copies:
        copy.start()
    core, chip = where[0], where[1]
    for level in range(2):
        window[2 * level + core] = mine[level]
        window[2 * level + 1 - core] = theirs[level]
    cut = parent_ref.shape[2]
    at = pl.ds(pl.multiple_of((chip * CORES + core) * cut, cut), cut)
    parent_ref[core] = own[:, at]
    parent_ref[1 - core] = theirs[0, :, at].astype(F32)
    for a in range(leaves):
        copies[a].wait()
        lhs = jnp.concatenate([window[targets[a, i]] for i in range(k)], axis=1)
        coupling = dot(lhs, blocks[a].reshape(k * wide, width))
        reduced = (solved[a].astype(F32) - coupling).astype(BF16)
        leaf_ref[a] = dot(reduced, upper[a])


def local(
    right_side, leaf_lower, leaf_upper, lower_blocks, upper_blocks, parent_rhs, parent_lower, parent_upper, targets
):
    rows, cols = lax.axis_size("row"), lax.axis_size("col")
    chips = cols // CORES
    here = lax.axis_index("col")
    core, chip = here % CORES, here // CORES
    where = jnp.stack([core, chip]).astype(jnp.int32)
    go = functools.partial(send, rows=rows, cols=cols)
    leaves, k, width, wide = lower_blocks.shape
    nrhs = right_side.shape[1]
    cut = parent_lower.shape[2]
    depth = cut * CORES

    upper_view = parent_upper.reshape(2, chips, depth, cut)
    lower_other = go(lax.dynamic_index_in_dim(parent_lower, 1 - core, 0, False), by_row=0, by_chip=0, flip=1)
    pieces = []
    for by in range(chips):
        for flip in range(CORES):
            if by == 0 and flip == 0:
                continue
            block = lax.dynamic_slice(
                upper_view, (core ^ flip, (chip + by) % chips, 0, 0), (1, 1, depth, cut)
            ).reshape(depth, cut)
            pieces.append(go(block, by_row=0, by_chip=by, flip=flip))

    solved, keep, give = pl.pallas_call(
        forward_kernel,
        in_specs=[SMEM, SMEM, ANY, ANY, ANY],
        out_specs=[VMEM, VMEM, VMEM],
        out_shape=[
            jax.ShapeDtypeStruct((leaves, nrhs, width), BF16),
            jax.ShapeDtypeStruct((2, nrhs, wide), F32),
            jax.ShapeDtypeStruct((2, nrhs, wide), BF16),
        ],
        scratch_shapes=[
            pltpu.VMEM(right_side.shape, BF16),
            pltpu.VMEM(leaf_lower.shape, BF16),
            pltpu.VMEM(lower_blocks.shape, BF16),
            pltpu.VMEM((4 * nrhs, wide), F32),
            pltpu.SemaphoreType.DMA((2 + leaves,)),
        ],
        compiler_params=pltpu.CompilerParams(vmem_limit_bytes=24 << 20),
        cost_estimate=pl.CostEstimate(flops=1 << 29, bytes_accessed=5 << 20, transcendentals=0),
        name="forward",
    )(where, targets, right_side, leaf_lower, lower_blocks)

    came = go(give, by_row=0, by_chip=0, flip=1)
    chip_sum = (keep + came.astype(F32)).astype(BF16)
    sums = [go(chip_sum[1], by_row=1, by_chip=by, flip=0) for by in range(chips)]
    sums += [go(chip_sum[0], by_row=0, by_chip=by, flip=0) for by in range(1, chips)]

    full, half = pl.pallas_call(
        functools.partial(parent_kernel, len(pieces), len(sums)),
        in_specs=[SMEM] + [VMEM] * (6 + len(pieces) + len(sums)),
        out_specs=[VMEM, VMEM],
        out_shape=[jax.ShapeDtypeStruct((nrhs, wide), F32), jax.ShapeDtypeStruct((nrhs, wide), BF16)],
        scratch_shapes=[pltpu.VMEM((nrhs, depth), BF16)],
        compiler_params=pltpu.CompilerParams(vmem_limit_bytes=24 << 20),
        cost_estimate=pl.CostEstimate(flops=1 << 27, bytes_accessed=4 << 20, transcendentals=0),
        name="parent",
    )(where, keep, came, parent_rhs, parent_lower, lower_other, parent_upper, *pieces, *sums)

    nexts = [go(half, by_row=-1, by_chip=by, flip=0) for by in range(chips)]
    own = full
    for by in range(1, chips):
        own = own + go(half, by_row=0, by_chip=by, flip=0).astype(F32)
    after = functools.reduce(jnp.add, [term.astype(F32) for term in nexts])
    mine = jnp.stack([own, after]).astype(BF16)
    theirs = go(mine, by_row=0, by_chip=0, flip=1)

    return pl.pallas_call(
        backward_kernel,
        in_specs=[SMEM, SMEM, VMEM, VMEM, VMEM, VMEM, ANY, VMEM],
        out_specs=[VMEM, VMEM],
        out_shape=[
            jax.ShapeDtypeStruct((leaves, nrhs, width), F32),
            jax.ShapeDtypeStruct((2, nrhs, cut), F32),
        ],
        scratch_shapes=[
            pltpu.VMEM((4, nrhs, wide), BF16),
            pltpu.VMEM(upper_blocks.shape, BF16),
            pltpu.SemaphoreType.DMA((leaves,)),
        ],
        compiler_params=pltpu.CompilerParams(vmem_limit_bytes=24 << 20),
        cost_estimate=pl.CostEstimate(flops=1 << 28, bytes_accessed=5 << 20, transcendentals=0),
        name="backward",
    )(where, targets, solved, own, mine, theirs, upper_blocks, leaf_upper)


def solution(mesh):
    placed = (
        P(("row", "col"), None, None),
        P(("row", "col"), None, None),
        P(("row", "col"), None, None),
        P(("row", "col"), None, None, None),
        P(("row", "col"), None, None, None),
        P("row", None, None),
        P("row", None, "col"),
        P("row", None, "col"),
        P(("row", "col"), None),
    )
    return jax.shard_map(
        local,
        mesh=mesh,
        in_specs=placed,
        out_specs=(P(("row", "col"), None, None), P("row", None, "col")),
        check_vma=False,
    )
```

```python
import functools

import jax
import jax.numpy as jnp
from jax import lax
from jax.experimental import pallas as pl
from jax.experimental.pallas import tpu as pltpu
from jax.sharding import PartitionSpec as P

CORES = 2
F32 = jnp.float32
BF16 = jnp.bfloat16
VMEM = pl.BlockSpec(memory_space=pltpu.VMEM)
SMEM = pl.BlockSpec(memory_space=pltpu.SMEM)
HBM = pl.BlockSpec(memory_space=pltpu.HBM)


def dot(a, b):
    return jnp.dot(a, b, preferred_element_type=F32)


def in_hbm(*arrays):
    return [pltpu.with_memory_space_constraint(array, pltpu.HBM) for array in arrays]


def in_vmem(*arrays):
    return [pltpu.with_memory_space_constraint(array, pltpu.VMEM) for array in arrays]


def place():
    here = lax.axis_index("col")
    return lax.rem(here, CORES), lax.div(here, CORES)


def send(array, rows, cols, by_row, by_chip, flip):
    chips = cols // CORES
    pairs = []
    for row in range(rows):
        for col in range(cols):
            chip, core = col // CORES, col % CORES
            to = ((chip + by_chip) % chips) * CORES + (core ^ flip)
            pairs.append((row * cols + col, ((row + by_row) % rows) * cols + to))
    return lax.ppermute(array, ("row", "col"), pairs)


def forward_kernel(chips, targets_hbm, rhs_hbm, lower_hbm, blocks_hbm, parent_lower, parent_upper, *rest):
    solved_ref, keep_ref, give_ref, across_ref, *piece_refs = rest[: 4 + CORES * (chips - 1)]
    targets, rhs, lower, blocks, acc, sems = rest[4 + CORES * (chips - 1) :]
    leaves, k, width, wide = blocks.shape
    nrhs = rhs.shape[1]
    depth = wide // chips
    core, chip = place()
    other = 1 - core
    first = [
        pltpu.make_async_copy(targets_hbm, targets, sems.at[0]),
        pltpu.make_async_copy(rhs_hbm, rhs, sems.at[1]),
        pltpu.make_async_copy(lower_hbm, lower, sems.at[2]),
    ]
    copies = [pltpu.make_async_copy(blocks_hbm.at[a], blocks.at[a], sems.at[3 + a]) for a in range(leaves)]

    def rows(by):
        return pl.ds(pl.multiple_of(lax.rem(chip + by, chips) * depth, depth), depth)

    moves = []
    for by in range(1, chips):
        for flip in range(CORES):
            moves.append((parent_upper.at[core if flip == 0 else other, rows(by), :], piece_refs[len(moves)]))
    moves.append((parent_lower.at[other], across_ref.at[pl.ds(0, wide)]))
    moves.append((parent_upper.at[other, rows(0), :], across_ref.at[pl.ds(wide, depth)]))
    last = [pltpu.make_async_copy(a, b, sems.at[3 + leaves + i]) for i, (a, b) in enumerate(moves)]
    for copy in first + copies + last:
        copy.start()
    slots = (core, 2 + core, other, 2 + other)
    for copy in first:
        copy.wait()
    solved = [dot(rhs[a], lower[a]).astype(BF16) for a in range(leaves)]
    for a in range(leaves):
        solved_ref[a] = solved[a]
    step = 2
    for a0 in range(0, leaves, step):
        lhs = jnp.concatenate(
            [
                jnp.concatenate(
                    [
                        jnp.where(targets[i, a] == slot, solved[a], jnp.zeros_like(solved[a]))
                        for a in range(a0, a0 + step)
                        for i in range(k)
                    ],
                    axis=1,
                )
                for slot in slots
            ],
            axis=0,
        )
        for a in range(a0, a0 + step):
            copies[a].wait()
        part = dot(lhs, blocks[pl.ds(a0, step)].reshape(step * k * width, wide))
        if a0 == 0:
            acc[...] = part
        elif a0 + step < leaves:
            acc[...] += part
        else:
            total = acc[...] + part
            keep_ref[...] = total[: 2 * nrhs].reshape(2, nrhs, wide)
            give_ref[...] = total[2 * nrhs :].astype(BF16).reshape(2, nrhs, wide)
    for copy in last:
        copy.wait()


def parent_kernel(chips, keep, came, rhs, lower, upper, across, *rest):
    pieces = rest[: CORES * (chips - 1)]
    sums = rest[len(pieces) : len(pieces) + 2 * chips - 1]
    full_ref, half_ref, forward = rest[len(pieces) + len(sums) :]
    core, chip = place()
    other = 1 - core
    wide = lower.shape[1]
    cut = lower.shape[2]
    depth = forward.shape[1]
    update = keep[0] + came[0].astype(F32)
    for term in sums:
        update = update + term[...].astype(F32)
    combined = (rhs[core].astype(F32) - update).astype(BF16)
    forward[:, pl.ds(pl.multiple_of(core * cut, cut), cut)] = dot(combined, lower[core]).astype(BF16)
    forward[:, pl.ds(pl.multiple_of(other * cut, cut), cut)] = dot(combined, across[pl.ds(0, wide)]).astype(BF16)
    lhs = forward[...]
    rows = pl.ds(pl.multiple_of(chip * depth, depth), depth)
    blocks = [(0, core, upper[core, rows, :]), (0, other, across[pl.ds(wide, depth)])]
    for by in range(1, chips):
        for flip in range(CORES):
            blocks.append((by, core if flip == 0 else other, pieces[len(blocks) - CORES][...]))
    for by, source_core, block in blocks:
        source = lax.rem(chip + chips - by, chips) * CORES + source_core
        part = dot(lhs, block)
        at = pl.ds(pl.multiple_of(source * cut, cut), cut)
        full_ref[:, at] = part
        half_ref[:, at] = part.astype(BF16)


def backward_kernel(targets, solved, own, mine, theirs, blocks, upper, leaf_ref, parent_ref, window):
    leaves, k, wide, width = blocks.shape
    core, chip = place()
    for level in range(2):
        window[2 * level + core] = mine[level]
        window[2 * level + 1 - core] = theirs[level]
    cut = parent_ref.shape[2]
    at = pl.ds(pl.multiple_of((chip * CORES + core) * cut, cut), cut)
    parent_ref[core] = own[:, at]
    parent_ref[1 - core] = theirs[0, :, at].astype(F32)
    for a in range(leaves):
        lhs = jnp.concatenate([window[targets[i, a]] for i in range(k)], axis=1)
        coupling = dot(lhs, blocks[a].reshape(k * wide, width))
        reduced = (solved[a].astype(F32) - coupling).astype(BF16)
        leaf_ref[a] = dot(reduced, upper[a])


def local(
    right_side, leaf_lower, leaf_upper, lower_blocks, upper_blocks, parent_rhs, parent_lower, parent_upper, targets
):
    rows, cols = lax.axis_size("row"), lax.axis_size("col")
    chips = cols // CORES
    go = functools.partial(send, rows=rows, cols=cols)
    leaves, k, width, wide = lower_blocks.shape
    nrhs = right_side.shape[1]
    cut = parent_lower.shape[2]
    depth = cut * CORES
    listed = targets.T

    n_pieces = CORES * (chips - 1)
    solved, keep, give, across, *pieces = pl.pallas_call(
        functools.partial(forward_kernel, chips),
        in_specs=[HBM] * 6,
        out_specs=[VMEM] * (4 + n_pieces),
        out_shape=[
            jax.ShapeDtypeStruct((leaves, nrhs, width), BF16),
            jax.ShapeDtypeStruct((2, nrhs, wide), F32),
            jax.ShapeDtypeStruct((2, nrhs, wide), BF16),
            jax.ShapeDtypeStruct((wide + depth, cut), BF16),
        ]
        + [jax.ShapeDtypeStruct((depth, cut), BF16)] * n_pieces,
        scratch_shapes=[
            pltpu.SMEM(listed.shape, jnp.int32),
            pltpu.VMEM(right_side.shape, BF16),
            pltpu.VMEM(leaf_lower.shape, BF16),
            pltpu.VMEM(lower_blocks.shape, BF16),
            pltpu.VMEM((4 * nrhs, wide), F32),
            pltpu.SemaphoreType.DMA((3 + leaves + n_pieces + 2,)),
        ],
        compiler_params=pltpu.CompilerParams(vmem_limit_bytes=24 << 20),
        cost_estimate=pl.CostEstimate(flops=1 << 29, bytes_accessed=5 << 20, transcendentals=0),
        name="forward",
    )(*in_hbm(listed, right_side, leaf_lower, lower_blocks, parent_lower, parent_upper))

    came = go(give, by_row=0, by_chip=0, flip=1)
    across = go(across, by_row=0, by_chip=0, flip=1)
    pieces = [
        go(piece, by_row=0, by_chip=1 + i // CORES, flip=i % CORES) for i, piece in enumerate(pieces)
    ]
    came, across = lax.optimization_barrier((came, across))
    chip_sum = (keep + came.astype(F32)).astype(BF16)
    sums = [go(chip_sum[1], by_row=1, by_chip=by, flip=0) for by in range(chips)]
    sums += [go(chip_sum[0], by_row=0, by_chip=by, flip=0) for by in range(1, chips)]

    full, half = pl.pallas_call(
        functools.partial(parent_kernel, chips),
        in_specs=[VMEM] * (6 + n_pieces + len(sums)),
        out_specs=[VMEM, VMEM],
        out_shape=[jax.ShapeDtypeStruct((nrhs, wide), F32), jax.ShapeDtypeStruct((nrhs, wide), BF16)],
        scratch_shapes=[pltpu.VMEM((nrhs, depth), BF16)],
        compiler_params=pltpu.CompilerParams(vmem_limit_bytes=24 << 20),
        cost_estimate=pl.CostEstimate(flops=1 << 27, bytes_accessed=4 << 20, transcendentals=0),
        name="parent",
    )(keep, came, parent_rhs, parent_lower, parent_upper, across, *pieces, *sums)

    nexts = [go(half, by_row=-1, by_chip=by, flip=0) for by in range(chips)]
    own = full
    for by in range(1, chips):
        own = own + go(half, by_row=0, by_chip=by, flip=0).astype(F32)
    after = functools.reduce(jnp.add, [term.astype(F32) for term in nexts])
    mine = jnp.stack([own, after]).astype(BF16)
    theirs = go(mine, by_row=0, by_chip=0, flip=1)

    return pl.pallas_call(
        backward_kernel,
        in_specs=[SMEM] + [VMEM] * 6,
        out_specs=[VMEM, VMEM],
        out_shape=[
            jax.ShapeDtypeStruct((leaves, nrhs, width), F32),
            jax.ShapeDtypeStruct((2, nrhs, cut), F32),
        ],
        scratch_shapes=[pltpu.VMEM((4, nrhs, wide), BF16)],
        compiler_params=pltpu.CompilerParams(vmem_limit_bytes=24 << 20),
        cost_estimate=pl.CostEstimate(flops=1 << 28, bytes_accessed=5 << 20, transcendentals=0),
        name="backward",
    )(listed, solved, own, mine, theirs, upper_blocks, leaf_upper)


def solution(mesh):
    placed = (
        P(("row", "col"), None, None),
        P(("row", "col"), None, None),
        P(("row", "col"), None, None),
        P(("row", "col"), None, None, None),
        P(("row", "col"), None, None, None),
        P("row", None, None),
        P("row", None, "col"),
        P("row", None, "col"),
        P(("row", "col"), None),
    )
    return jax.shard_map(
        local,
        mesh=mesh,
        in_specs=placed,
        out_specs=(P(("row", "col"), None, None), P("row", None, "col")),
        check_vma=False,
    )
```

```python
import functools

import jax
import jax.numpy as jnp
from jax import lax
from jax.experimental import pallas as pl
from jax.experimental.pallas import tpu as pltpu
from jax.sharding import PartitionSpec as P

CORES = 2
F32 = jnp.float32
BF16 = jnp.bfloat16
VMEM = pl.BlockSpec(memory_space=pltpu.VMEM)
SMEM = pl.BlockSpec(memory_space=pltpu.SMEM)
HBM = pl.BlockSpec(memory_space=pltpu.HBM)


def dot(a, b):
    return jnp.dot(a, b, preferred_element_type=F32)


def in_hbm(*arrays):
    return [pltpu.with_memory_space_constraint(array, pltpu.HBM) for array in arrays]


def in_vmem(*arrays):
    return [pltpu.with_memory_space_constraint(array, pltpu.VMEM) for array in arrays]


def place():
    here = lax.axis_index("col")
    return lax.rem(here, CORES), lax.div(here, CORES)


def send(array, rows, cols, by_row, by_chip, flip):
    chips = cols // CORES
    pairs = []
    for row in range(rows):
        for col in range(cols):
            chip, core = col // CORES, col % CORES
            to = ((chip + by_chip) % chips) * CORES + (core ^ flip)
            pairs.append((row * cols + col, ((row + by_row) % rows) * cols + to))
    return lax.ppermute(array, ("row", "col"), pairs)


def forward_kernel(targets_hbm, rhs_hbm, lower_hbm, blocks_hbm, parent_lower, parent_upper, *rest):
    solved_ref, keep_ref, give_ref, across_ref, targets, rhs, lower, blocks, acc, sems = rest
    leaves, k, width, wide = blocks.shape
    nrhs = rhs.shape[1]
    core, _ = place()
    other = 1 - core
    first = [
        pltpu.make_async_copy(targets_hbm, targets, sems.at[0]),
        pltpu.make_async_copy(rhs_hbm, rhs, sems.at[1]),
        pltpu.make_async_copy(lower_hbm, lower, sems.at[2]),
    ]
    copies = [pltpu.make_async_copy(blocks_hbm.at[a], blocks.at[a], sems.at[3 + a]) for a in range(leaves)]
    last = [
        pltpu.make_async_copy(parent_lower.at[other], across_ref.at[0], sems.at[3 + leaves]),
        pltpu.make_async_copy(parent_upper.at[other], across_ref.at[1], sems.at[4 + leaves]),
    ]
    for copy in first + copies + last:
        copy.start()
    slots = (core, 2 + core, other, 2 + other)
    for copy in first:
        copy.wait()
    solved = [dot(rhs[a], lower[a]).astype(BF16) for a in range(leaves)]
    for a in range(leaves):
        solved_ref[a] = solved[a]
    step = 2
    for a0 in range(0, leaves, step):
        lhs = jnp.concatenate(
            [
                jnp.concatenate(
                    [
                        jnp.where(targets[i, a] == slot, solved[a], jnp.zeros_like(solved[a]))
                        for a in range(a0, a0 + step)
                        for i in range(k)
                    ],
                    axis=1,
                )
                for slot in slots
            ],
            axis=0,
        )
        for a in range(a0, a0 + step):
            copies[a].wait()
        part = dot(lhs, blocks[pl.ds(a0, step)].reshape(step * k * width, wide))
        if a0 == 0:
            acc[...] = part
        elif a0 + step < leaves:
            acc[...] += part
        else:
            total = acc[...] + part
            keep_ref[...] = total[: 2 * nrhs].reshape(2, nrhs, wide)
            give_ref[...] = total[2 * nrhs :].astype(BF16).reshape(2, nrhs, wide)
    for copy in last:
        copy.wait()


def parent_forward_kernel(keep, came, rhs, lower, across, *rest):
    sums, half_ref = rest[:-1], rest[-1]
    core, _ = place()
    other = 1 - core
    cut = lower.shape[2]
    update = keep[0] + came[0].astype(F32)
    for term in sums:
        update = update + term[...].astype(F32)
    combined = (rhs[core].astype(F32) - update).astype(BF16)
    half_ref[:, pl.ds(pl.multiple_of(core * cut, cut), cut)] = dot(combined, lower[core]).astype(BF16)
    half_ref[:, pl.ds(pl.multiple_of(other * cut, cut), cut)] = dot(combined, across[0]).astype(BF16)


def parent_backward_kernel(upper, across, *rest):
    halves, (full_ref, half_ref, forward) = rest[:-3], rest[-3:]
    chips = len(halves)
    core, chip = place()
    other = 1 - core
    cut = upper.shape[2]
    depth = halves[0].shape[1]
    for by, half in enumerate(halves):
        source = lax.rem(chip + chips - by, chips)
        forward[:, pl.ds(pl.multiple_of(source * depth, depth), depth)] = half[...]
    for at, block in ((core, upper[core]), (other, across[1])):
        part = dot(forward[...], block)
        at = pl.ds(pl.multiple_of(at * cut, cut), cut)
        full_ref[:, at] = part
        half_ref[:, at] = part.astype(BF16)


def backward_kernel(targets, solved, own, mine, theirs, blocks, upper, leaf_ref, parent_ref, window):
    leaves, k, wide, width = blocks.shape
    chips, depth = mine.shape[1], mine.shape[3]
    core, chip = place()
    for by in range(chips):
        source = lax.rem(chip + chips - by, chips)
        at = pl.ds(pl.multiple_of(source * depth, depth), depth)
        for level in range(2):
            window[2 * level + core, :, at] = mine[level, by]
            window[2 * level + 1 - core, :, at] = theirs[level, by]
    cut = parent_ref.shape[2]
    at = pl.ds(pl.multiple_of(core * cut, cut), cut)
    parent_ref[core] = own[:, at]
    parent_ref[1 - core] = theirs[0, 0, :, at].astype(F32)
    for a in range(leaves):
        lhs = jnp.concatenate([window[targets[i, a]] for i in range(k)], axis=1)
        coupling = dot(lhs, blocks[a].reshape(k * wide, width))
        reduced = (solved[a].astype(F32) - coupling).astype(BF16)
        leaf_ref[a] = dot(reduced, upper[a])


def local(
    right_side, leaf_lower, leaf_upper, lower_blocks, upper_blocks, parent_rhs, parent_lower, parent_upper, targets
):
    rows, cols = lax.axis_size("row"), lax.axis_size("col")
    chips = cols // CORES
    go = functools.partial(send, rows=rows, cols=cols)
    leaves, k, width, wide = lower_blocks.shape
    nrhs = right_side.shape[1]
    cut = parent_lower.shape[2]
    depth = cut * CORES
    listed = targets.T

    solved, keep, give, across = pl.pallas_call(
        forward_kernel,
        in_specs=[HBM] * 6,
        out_specs=[VMEM] * 4,
        out_shape=[
            jax.ShapeDtypeStruct((leaves, nrhs, width), BF16),
            jax.ShapeDtypeStruct((2, nrhs, wide), F32),
            jax.ShapeDtypeStruct((2, nrhs, wide), BF16),
            jax.ShapeDtypeStruct((2, wide, cut), BF16),
        ],
        scratch_shapes=[
            pltpu.SMEM(listed.shape, jnp.int32),
            pltpu.VMEM(right_side.shape, BF16),
            pltpu.VMEM(leaf_lower.shape, BF16),
            pltpu.VMEM(lower_blocks.shape, BF16),
            pltpu.VMEM((4 * nrhs, wide), F32),
            pltpu.SemaphoreType.DMA((5 + leaves,)),
        ],
        compiler_params=pltpu.CompilerParams(vmem_limit_bytes=24 << 20),
        cost_estimate=pl.CostEstimate(flops=1 << 29, bytes_accessed=5 << 20, transcendentals=0),
        name="forward",
    )(*in_hbm(listed, right_side, leaf_lower, lower_blocks, parent_lower, parent_upper))

    came = go(give, by_row=0, by_chip=0, flip=1)
    came, across = lax.optimization_barrier((came, across))
    across = go(across, by_row=0, by_chip=0, flip=1)
    chip_sum = (keep + came.astype(F32)).astype(BF16)
    sums = [go(chip_sum[1], by_row=1, by_chip=by, flip=0) for by in range(chips)]
    sums += [go(chip_sum[0], by_row=0, by_chip=by, flip=0) for by in range(1, chips)]

    half = pl.pallas_call(
        parent_forward_kernel,
        in_specs=[VMEM] * (5 + len(sums)),
        out_specs=VMEM,
        out_shape=jax.ShapeDtypeStruct((nrhs, depth), BF16),
        compiler_params=pltpu.CompilerParams(vmem_limit_bytes=16 << 20),
        cost_estimate=pl.CostEstimate(flops=1 << 25, bytes_accessed=2 << 20, transcendentals=0),
        name="parent_forward",
    )(keep, came, parent_rhs, parent_lower, across, *sums)
    halves = [half] + [go(half, by_row=0, by_chip=by, flip=0) for by in range(1, chips)]

    full, half = pl.pallas_call(
        parent_backward_kernel,
        in_specs=[VMEM] * (2 + chips),
        out_specs=[VMEM, VMEM],
        out_shape=[jax.ShapeDtypeStruct((nrhs, depth), F32), jax.ShapeDtypeStruct((nrhs, depth), BF16)],
        scratch_shapes=[pltpu.VMEM((nrhs, wide), BF16)],
        compiler_params=pltpu.CompilerParams(vmem_limit_bytes=16 << 20),
        cost_estimate=pl.CostEstimate(flops=1 << 25, bytes_accessed=2 << 20, transcendentals=0),
        name="parent_backward",
    )(parent_upper, across, *halves)

    nexts = [go(half, by_row=-1, by_chip=by, flip=0) for by in range(chips)]
    owns = [half] + [go(half, by_row=0, by_chip=by, flip=0) for by in range(1, chips)]
    mine = jnp.stack([jnp.stack(owns), jnp.stack(nexts)])
    theirs = go(mine, by_row=0, by_chip=0, flip=1)

    return pl.pallas_call(
        backward_kernel,
        in_specs=[SMEM] + [VMEM] * 6,
        out_specs=[VMEM, VMEM],
        out_shape=[
            jax.ShapeDtypeStruct((leaves, nrhs, width), F32),
            jax.ShapeDtypeStruct((2, nrhs, cut), F32),
        ],
        scratch_shapes=[pltpu.VMEM((4, nrhs, wide), BF16)],
        compiler_params=pltpu.CompilerParams(vmem_limit_bytes=24 << 20),
        cost_estimate=pl.CostEstimate(flops=1 << 28, bytes_accessed=5 << 20, transcendentals=0),
        name="backward",
    )(listed, solved, full, mine, theirs, upper_blocks, leaf_upper)


def solution(mesh):
    placed = (
        P(("row", "col"), None, None),
        P(("row", "col"), None, None),
        P(("row", "col"), None, None),
        P(("row", "col"), None, None, None),
        P(("row", "col"), None, None, None),
        P("row", None, None),
        P("row", None, "col"),
        P("row", None, "col"),
        P(("row", "col"), None),
    )
    return jax.shard_map(
        local,
        mesh=mesh,
        in_specs=placed,
        out_specs=(P(("row", "col"), None, None), P("row", None, "col")),
        check_vma=False,
    )
```

```python
import functools

import jax
import jax.numpy as jnp
from jax import lax
from jax.experimental import pallas as pl
from jax.experimental.pallas import tpu as pltpu
from jax.sharding import PartitionSpec as P

CORES = 2
F32 = jnp.float32
BF16 = jnp.bfloat16
VMEM = pl.BlockSpec(memory_space=pltpu.VMEM)
HBM = pl.BlockSpec(memory_space=pltpu.HBM)


def dot(a, b):
    return jnp.dot(a, b, preferred_element_type=F32)


def in_hbm(*arrays):
    return [pltpu.with_memory_space_constraint(array, pltpu.HBM) for array in arrays]


def place():
    here = lax.axis_index("col")
    chip, core = lax.div(here, CORES), lax.rem(here, CORES)
    return chip, core, lax.rem(chip + core, CORES)


def send(array, rows, cols, by_row, by_chip, other):
    chips = cols // CORES
    pairs = []
    for row in range(rows):
        for col in range(cols):
            chip, core = col // CORES, col % CORES
            to_chip = (chip + by_chip) % chips
            to_core = (chip + core + to_chip + other) % CORES
            pairs.append((row * cols + col, ((row + by_row) % rows) * cols + to_chip * CORES + to_core))
    return lax.ppermute(array, ("row", "col"), pairs)


def columns(index, size):
    return pl.ds(pl.multiple_of(index * size, size), size)


def forward_kernel(targets_hbm, rhs_hbm, lower_hbm, blocks_hbm, solved_ref, keep_ref, give_ref, targets, rhs, lower, blocks, acc, sems):
    leaves, k, width, wide = blocks.shape
    nrhs = rhs.shape[1]
    _, _, parent = place()
    first = [
        pltpu.make_async_copy(targets_hbm, targets, sems.at[0]),
        pltpu.make_async_copy(rhs_hbm, rhs, sems.at[1]),
        pltpu.make_async_copy(lower_hbm, lower, sems.at[2]),
    ]
    copies = [pltpu.make_async_copy(blocks_hbm.at[a], blocks.at[a], sems.at[3 + a]) for a in range(leaves)]
    for copy in first + copies:
        copy.start()
    windows = (parent, 2 + parent, 3 - parent, 1 - parent)
    for copy in first:
        copy.wait()
    solved = [dot(rhs[a], lower[a]).astype(BF16) for a in range(leaves)]
    for a in range(leaves):
        solved_ref[a] = solved[a]
    for a in range(leaves):
        lhs = jnp.concatenate(
            [
                jnp.concatenate(
                    [jnp.where(targets[i, a] == window, solved[a], jnp.zeros_like(solved[a])) for i in range(k)], axis=1
                )
                for window in windows
            ],
            axis=0,
        )
        copies[a].wait()
        part = dot(lhs, blocks[a].reshape(k * width, wide))
        if a == 0:
            acc[...] = part
        elif a + 1 < leaves:
            acc[...] += part
        else:
            total = acc[...] + part
            keep_ref[...] = total[: 3 * nrhs].reshape(3, nrhs, wide)
            give_ref[...] = total[nrhs:].astype(BF16).reshape(3, nrhs, wide)


def parent_forward_kernel(keep, came, rhs, lower, across, *rest):
    sums, half_ref = rest[:-1], rest[-1]
    _, core, parent = place()
    cut = lower.shape[2]
    update = keep[0] + came[2].astype(F32)
    for term in sums:
        update = update + term[...].astype(F32)
    combined = (rhs[parent].astype(F32) - update).astype(BF16)
    half_ref[:, columns(core, cut)] = dot(combined, lower[parent]).astype(BF16)
    half_ref[:, columns(1 - core, cut)] = dot(combined, across[0]).astype(BF16)


def parent_backward_kernel(upper, across, *rest):
    halves, (full_ref, half_ref, forward) = rest[:-3], rest[-3:]
    chips = len(halves)
    chip, core, parent = place()
    cut = upper.shape[2]
    for by, half in enumerate(halves):
        forward[:, columns(lax.rem(chip + chips - by, chips), half.shape[1])] = half[...]
    for at, block in ((core, upper[parent]), (1 - core, across[1])):
        part = dot(forward[...], block)
        full_ref[:, columns(at, cut)] = part
        half_ref[:, columns(at, cut)] = part.astype(BF16)


def backward_kernel(flows, targets, solved, own, mine, theirs, blocks, upper, leaf_ref, parent_ref, window):
    leaves, k, wide, width = blocks.shape
    depth = mine.shape[2]
    chips = wide // depth
    chip, core, parent = place()
    for i, (level, by) in enumerate(flows):
        at = columns(lax.rem(chip + chips - by, chips), depth)
        of = lax.rem(parent + level * (by + 1), CORES)
        window[CORES * level + of, :, at] = mine[i]
        window[CORES * level + 1 - of, :, at] = theirs[i]
    cut = parent_ref.shape[2]
    parent_ref[parent] = own[:, columns(core, cut)]
    parent_ref[1 - parent] = theirs[flows.index((0, 0)), :, columns(core, cut)].astype(F32)
    listed = targets[...]
    couplings = [
        functools.reduce(jnp.add, [dot(window[listed[i, a]], blocks[a, i]) for i in range(k)]) for a in range(leaves)
    ]
    for a in range(leaves):
        reduced = (solved[a].astype(F32) - couplings[a]).astype(BF16)
        leaf_ref[a] = dot(reduced, upper[a])


def local(
    right_side, leaf_lower, leaf_upper, lower_blocks, upper_blocks, parent_rhs, parent_lower, parent_upper, targets
):
    rows, cols = lax.axis_size("row"), lax.axis_size("col")
    chips = cols // CORES
    go = functools.partial(send, rows=rows, cols=cols)
    leaves, k, width, wide = lower_blocks.shape
    nrhs = right_side.shape[1]
    cut = parent_lower.shape[2]
    depth = cut * CORES
    listed = targets.T

    solved, keep, give = pl.pallas_call(
        forward_kernel,
        in_specs=[HBM] * 4,
        out_specs=[VMEM] * 3,
        out_shape=[
            jax.ShapeDtypeStruct((leaves, nrhs, width), BF16),
            jax.ShapeDtypeStruct((3, nrhs, wide), F32),
            jax.ShapeDtypeStruct((3, nrhs, wide), BF16),
        ],
        scratch_shapes=[
            pltpu.SMEM(listed.shape, jnp.int32),
            pltpu.VMEM(right_side.shape, BF16),
            pltpu.VMEM(leaf_lower.shape, BF16),
            pltpu.VMEM(lower_blocks.shape, BF16),
            pltpu.VMEM((4 * nrhs, wide), F32),
            pltpu.SemaphoreType.DMA((3 + leaves,)),
        ],
        compiler_params=pltpu.CompilerParams(vmem_limit_bytes=24 << 20),
        cost_estimate=pl.CostEstimate(flops=1 << 29, bytes_accessed=5 << 20, transcendentals=0),
        name="forward",
    )(*in_hbm(listed, right_side, leaf_lower, lower_blocks))

    give, lower_after, upper_after = lax.optimization_barrier((give, parent_lower, parent_upper))
    came = go(give, by_row=0, by_chip=0, other=1)
    _, _, parent = place()
    across = jnp.stack([lax.dynamic_index_in_dim(x, 1 - parent, 0, False) for x in (lower_after, upper_after)])
    came, across = lax.optimization_barrier((came, across))
    across = go(across, by_row=0, by_chip=0, other=1)
    own_sum = (keep[0] + came[2].astype(F32)).astype(BF16)
    next_sums = [(keep[1] + came[1].astype(F32)).astype(BF16), (keep[2] + came[0].astype(F32)).astype(BF16)]
    sums = [go(next_sums[(by + 1) % CORES], by_row=1, by_chip=by, other=(by + 1) % CORES) for by in range(chips)]
    sums += [go(own_sum, by_row=0, by_chip=by, other=0) for by in range(1, chips)]

    half = pl.pallas_call(
        parent_forward_kernel,
        in_specs=[VMEM] * (5 + len(sums)),
        out_specs=VMEM,
        out_shape=jax.ShapeDtypeStruct((nrhs, depth), BF16),
        compiler_params=pltpu.CompilerParams(vmem_limit_bytes=16 << 20),
        cost_estimate=pl.CostEstimate(flops=1 << 25, bytes_accessed=2 << 20, transcendentals=0),
        name="parent_forward",
    )(keep, came, parent_rhs, lower_after, across, *sums)
    halves = [half] + [go(half, by_row=0, by_chip=by, other=0) for by in range(1, chips)]

    full, half = pl.pallas_call(
        parent_backward_kernel,
        in_specs=[VMEM] * (2 + chips),
        out_specs=[VMEM, VMEM],
        out_shape=[jax.ShapeDtypeStruct((nrhs, depth), F32), jax.ShapeDtypeStruct((nrhs, depth), BF16)],
        scratch_shapes=[pltpu.VMEM((nrhs, wide), BF16)],
        compiler_params=pltpu.CompilerParams(vmem_limit_bytes=16 << 20),
        cost_estimate=pl.CostEstimate(flops=1 << 25, bytes_accessed=2 << 20, transcendentals=0),
        name="parent_backward",
    )(upper_after, across, *halves)

    flows = [(0, 0)] + [(1, by) for by in reversed(range(chips))] + [(0, by) for by in range(1, chips)]
    mine = jnp.stack(
        [
            half if flow == (0, 0) else go(half, by_row=-flow[0], by_chip=flow[1], other=flow[0] * (flow[1] + 1) % CORES)
            for flow in flows
        ]
    )
    theirs = go(mine, by_row=0, by_chip=0, other=1)

    return pl.pallas_call(
        functools.partial(backward_kernel, flows),
        in_specs=[VMEM] * 7,
        out_specs=[VMEM, VMEM],
        out_shape=[
            jax.ShapeDtypeStruct((leaves, nrhs, width), F32),
            jax.ShapeDtypeStruct((2, nrhs, cut), F32),
        ],
        scratch_shapes=[pltpu.VMEM((4, nrhs, wide), BF16)],
        compiler_params=pltpu.CompilerParams(vmem_limit_bytes=24 << 20),
        cost_estimate=pl.CostEstimate(flops=1 << 28, bytes_accessed=5 << 20, transcendentals=0),
        name="backward",
    )(listed, solved, full, mine, theirs, upper_blocks, leaf_upper)


def solution(mesh):
    placed = (
        P(("row", "col"), None, None),
        P(("row", "col"), None, None),
        P(("row", "col"), None, None),
        P(("row", "col"), None, None, None),
        P(("row", "col"), None, None, None),
        P("row", None, None),
        P("row", None, "col"),
        P("row", None, "col"),
        P(("row", "col"), None),
    )
    return jax.shard_map(
        local,
        mesh=mesh,
        in_specs=placed,
        out_specs=(P(("row", "col"), None, None), P("row", None, "col")),
        check_vma=False,
    )
```

```python
import functools

import jax
import jax.numpy as jnp
from jax import lax
from jax.experimental import pallas as pl
from jax.experimental.pallas import tpu as pltpu
from jax.sharding import PartitionSpec as P

CORES = 2
F32 = jnp.float32
BF16 = jnp.bfloat16
VMEM = pl.BlockSpec(memory_space=pltpu.VMEM)
HBM = pl.BlockSpec(memory_space=pltpu.HBM)


def dot(a, b):
    return jnp.dot(a, b, preferred_element_type=F32)


def in_hbm(*arrays):
    return [pltpu.with_memory_space_constraint(array, pltpu.HBM) for array in arrays]


def place():
    here = lax.axis_index("col")
    chip, core = lax.div(here, CORES), lax.rem(here, CORES)
    return chip, core, lax.rem(chip + core, CORES)


def send(array, rows, cols, by_row, target):
    chips = cols // CORES
    pairs = []
    for row in range(rows):
        for col in range(cols):
            chip, core = target(col // CORES, col % CORES)
            pairs.append((row * cols + col, ((row + by_row) % rows) * cols + chip % chips * CORES + core))
    return lax.ppermute(array, ("row", "col"), pairs)


def along(by, other=0):
    return lambda chip, core: (chip + by, (core + by + other) % CORES)


def fan(by):
    return lambda chip, core: (chip + by + core, core)


def columns(index, size):
    return pl.ds(pl.multiple_of(index * size, size), size)


def forward_kernel(targets_hbm, rhs_hbm, lower_hbm, blocks_hbm, solved_ref, keep_ref, give_ref, targets, rhs, lower, blocks, acc, sems):
    leaves, k, width, wide = blocks.shape
    nrhs = rhs.shape[1]
    _, _, parent = place()
    first = [
        pltpu.make_async_copy(targets_hbm, targets, sems.at[0]),
        pltpu.make_async_copy(rhs_hbm, rhs, sems.at[1]),
        pltpu.make_async_copy(lower_hbm, lower, sems.at[2]),
    ]
    copies = [pltpu.make_async_copy(blocks_hbm.at[a], blocks.at[a], sems.at[3 + a]) for a in range(leaves)]
    for copy in first + copies:
        copy.start()
    windows = (parent, 2 + parent, 3 - parent, 1 - parent)
    for copy in first:
        copy.wait()
    solved = [dot(rhs[a], lower[a]).astype(BF16) for a in range(leaves)]
    for a in range(leaves):
        solved_ref[a] = solved[a]
    for a in range(leaves):
        lhs = jnp.concatenate(
            [
                jnp.concatenate(
                    [jnp.where(targets[i, a] == window, solved[a], jnp.zeros_like(solved[a])) for i in range(k)], axis=1
                )
                for window in windows
            ],
            axis=0,
        )
        copies[a].wait()
        part = dot(lhs, blocks[a].reshape(k * width, wide))
        if a == 0:
            acc[...] = part
        elif a + 1 < leaves:
            acc[...] += part
        else:
            total = acc[...] + part
            keep_ref[...] = total[: 3 * nrhs].reshape(3, nrhs, wide)
            give_ref[...] = total[nrhs:].astype(BF16).reshape(3, nrhs, wide)


def parent_forward_kernel(keep, came, rhs, lower, across, *rest):
    sums, half_ref = rest[:-1], rest[-1]
    _, core, parent = place()
    cut = lower.shape[2]
    update = keep[0] + came[2].astype(F32)
    for term in sums:
        update = update + term[...].astype(F32)
    combined = (rhs[parent].astype(F32) - update).astype(BF16)
    half_ref[:, columns(core, cut)] = dot(combined, lower[parent]).astype(BF16)
    half_ref[:, columns(1 - core, cut)] = dot(combined, across[0]).astype(BF16)


def parent_backward_kernel(upper, across, *rest):
    mine, theirs, parent_ref, half_ref, forward = rest
    chips = mine.shape[0]
    chip, core, parent = place()
    cut = upper.shape[2]
    for by in range(chips):
        at = columns(lax.rem(chip + chips - by, chips), mine.shape[2])
        forward[parent, :, at] = mine[by]
        forward[1 - parent, :, at] = theirs[by]
    for this in range(CORES):
        part = dot(forward[this], upper[this])
        parent_ref[this] = part
        half_ref[this, :, columns(core, cut)] = part.astype(BF16)
        half_ref[this, :, columns(1 - core, cut)] = dot(forward[this], across[1 + this]).astype(BF16)


def backward_kernel(targets, full, solved, mine, theirs, blocks, upper, *rest):
    halves, (leaf_ref, parent_ref, window) = rest[:-3], rest[-3:]
    parent_ref[...] = full[...]
    leaves, k, wide, width = blocks.shape
    chips = len(halves)
    depth = wide // chips
    chip, core, _ = place()
    for by, half in enumerate(halves):
        window[pl.ds(0, 2), :, columns(lax.rem(chip + chips - by, chips), depth)] = half[...]
    for by in range(0, chips, CORES):
        for arrived, lag in ((mine, core), (theirs, 1 - core)):
            at = columns(lax.rem(chip + chips - by - lag, chips), depth)
            window[pl.ds(2, 2), :, at] = arrived[by // CORES]
    listed = targets[...]
    couplings = [
        functools.reduce(jnp.add, [dot(window[listed[i, a]], blocks[a, i]) for i in range(k)]) for a in range(leaves)
    ]
    for a in range(leaves):
        reduced = (solved[a].astype(F32) - couplings[a]).astype(BF16)
        leaf_ref[a] = dot(reduced, upper[a])


def local(
    right_side, leaf_lower, leaf_upper, lower_blocks, upper_blocks, parent_rhs, parent_lower, parent_upper, targets
):
    rows, cols = lax.axis_size("row"), lax.axis_size("col")
    chips = cols // CORES
    go = functools.partial(send, rows=rows, cols=cols)
    leaves, k, width, wide = lower_blocks.shape
    nrhs = right_side.shape[1]
    cut = parent_lower.shape[2]
    depth = cut * CORES
    listed = targets.T

    solved, keep, give = pl.pallas_call(
        forward_kernel,
        in_specs=[HBM] * 4,
        out_specs=[VMEM] * 3,
        out_shape=[
            jax.ShapeDtypeStruct((leaves, nrhs, width), BF16),
            jax.ShapeDtypeStruct((3, nrhs, wide), F32),
            jax.ShapeDtypeStruct((3, nrhs, wide), BF16),
        ],
        scratch_shapes=[
            pltpu.SMEM(listed.shape, jnp.int32),
            pltpu.VMEM(right_side.shape, BF16),
            pltpu.VMEM(leaf_lower.shape, BF16),
            pltpu.VMEM(lower_blocks.shape, BF16),
            pltpu.VMEM((4 * nrhs, wide), F32),
            pltpu.SemaphoreType.DMA((3 + leaves,)),
        ],
        compiler_params=pltpu.CompilerParams(vmem_limit_bytes=24 << 20),
        cost_estimate=pl.CostEstimate(flops=1 << 29, bytes_accessed=5 << 20, transcendentals=0),
        name="forward",
    )(*in_hbm(listed, right_side, leaf_lower, lower_blocks))

    give, lower, upper = lax.optimization_barrier((give, parent_lower, parent_upper))
    came = go(give, by_row=0, target=along(0, 1))
    _, _, parent = place()
    across = jnp.concatenate([lax.dynamic_index_in_dim(lower, 1 - parent, 0), upper])
    came, across = lax.optimization_barrier((came, across))
    across = go(across, by_row=0, target=along(0, 1))
    own_sum = (keep[0] + came[2].astype(F32)).astype(BF16)
    next_sums = [(keep[1] + came[1].astype(F32)).astype(BF16), (keep[2] + came[0].astype(F32)).astype(BF16)]
    sums = [
        go(next_sums[(by + 1) % CORES], by_row=1, target=along(by, (by + 1) % CORES)) for by in reversed(range(chips))
    ]
    sums += [go(own_sum, by_row=0, target=along(by)) for by in range(1, chips)]

    half = pl.pallas_call(
        parent_forward_kernel,
        in_specs=[VMEM] * (5 + len(sums)),
        out_specs=VMEM,
        out_shape=jax.ShapeDtypeStruct((nrhs, depth), BF16),
        compiler_params=pltpu.CompilerParams(vmem_limit_bytes=16 << 20),
        cost_estimate=pl.CostEstimate(flops=1 << 25, bytes_accessed=2 << 20, transcendentals=0),
        name="parent_forward",
    )(keep, came, parent_rhs, lower, across, *sums)
    halves = jnp.stack([half] + [go(half, by_row=0, target=along(by)) for by in range(1, chips)])
    halves = (halves, go(halves, by_row=0, target=along(0, 1)))

    full, half = pl.pallas_call(
        parent_backward_kernel,
        in_specs=[VMEM] * (2 + len(halves)),
        out_specs=[VMEM, VMEM],
        out_shape=[jax.ShapeDtypeStruct((2, nrhs, cut), F32), jax.ShapeDtypeStruct((2, nrhs, depth), BF16)],
        scratch_shapes=[pltpu.VMEM((2, nrhs, wide), BF16)],
        compiler_params=pltpu.CompilerParams(vmem_limit_bytes=16 << 20),
        cost_estimate=pl.CostEstimate(flops=1 << 26, bytes_accessed=4 << 20, transcendentals=0),
        name="parent_backward",
    )(upper, across, *halves)

    halves = [half] + [go(half, by_row=0, target=along(by, (by + 1) % CORES)) for by in range(1, chips)]
    mine = jnp.stack([go(half, by_row=-1, target=fan(by)) for by in range(0, chips, CORES)])
    theirs = go(mine, by_row=0, target=along(0, 1))

    return pl.pallas_call(
        backward_kernel,
        in_specs=[VMEM] * (7 + chips),
        out_specs=[VMEM, VMEM],
        out_shape=[jax.ShapeDtypeStruct((leaves, nrhs, width), F32), jax.ShapeDtypeStruct(full.shape, F32)],
        scratch_shapes=[pltpu.VMEM((4, nrhs, wide), BF16)],
        compiler_params=pltpu.CompilerParams(vmem_limit_bytes=24 << 20),
        cost_estimate=pl.CostEstimate(flops=1 << 28, bytes_accessed=5 << 20, transcendentals=0),
        name="backward",
    )(listed, full, solved, mine, theirs, upper_blocks, leaf_upper, *halves)


def solution(mesh):
    placed = (
        P(("row", "col"), None, None),
        P(("row", "col"), None, None),
        P(("row", "col"), None, None),
        P(("row", "col"), None, None, None),
        P(("row", "col"), None, None, None),
        P("row", None, None),
        P("row", None, "col"),
        P("row", None, "col"),
        P(("row", "col"), None),
    )
    return jax.shard_map(
        local,
        mesh=mesh,
        in_specs=placed,
        out_specs=(P(("row", "col"), None, None), P("row", None, "col")),
        check_vma=False,
    )
```

```python
import functools

import jax
import jax.numpy as jnp
from jax import lax
from jax.experimental import pallas as pl
from jax.experimental.pallas import tpu as pltpu
from jax.sharding import PartitionSpec as P

CORES = 2
F32 = jnp.float32
BF16 = jnp.bfloat16
VMEM = pl.BlockSpec(memory_space=pltpu.VMEM)
HBM = pl.BlockSpec(memory_space=pltpu.HBM)


def dot(a, b):
    return jnp.dot(a, b, preferred_element_type=F32)


def in_hbm(*arrays):
    return [pltpu.with_memory_space_constraint(array, pltpu.HBM) for array in arrays]


def place():
    here = lax.axis_index("col")
    chip, core = lax.div(here, CORES), lax.rem(here, CORES)
    return chip, core, lax.rem(chip + core, CORES)


def send(array, rows, cols, by_row, target):
    chips = cols // CORES
    pairs = []
    for row in range(rows):
        for col in range(cols):
            chip, core = target(col // CORES, col % CORES)
            pairs.append((row * cols + col, ((row + by_row) % rows) * cols + chip % chips * CORES + core))
    return lax.ppermute(array, ("row", "col"), pairs)


def along(by, other=0):
    return lambda chip, core: (chip + by, (core + by + other) % CORES)


def fan(by):
    return lambda chip, core: (chip + by + core, core)


def columns(index, size):
    return pl.ds(pl.multiple_of(index * size, size), size)


def forward_kernel(targets_hbm, rhs_hbm, lower_hbm, blocks_hbm, solved_ref, keep_ref, give_ref, targets, rhs, lower, blocks, acc, sems):
    leaves, k, width, wide = blocks.shape
    nrhs = rhs.shape[1]
    _, _, parent = place()
    first = [
        pltpu.make_async_copy(targets_hbm, targets, sems.at[0]),
        pltpu.make_async_copy(rhs_hbm, rhs, sems.at[1]),
        pltpu.make_async_copy(lower_hbm, lower, sems.at[2]),
    ]
    copies = [pltpu.make_async_copy(blocks_hbm.at[a], blocks.at[a], sems.at[3 + a]) for a in range(leaves)]
    for copy in first + copies:
        copy.start()
    windows = (parent, 3 - parent, 1 - parent, 2 + parent)
    for copy in first:
        copy.wait()
    solved = [dot(rhs[a], lower[a]).astype(BF16) for a in range(leaves)]
    for a in range(leaves):
        solved_ref[a] = solved[a]
    for a in range(leaves):
        lhs = jnp.concatenate(
            [
                jnp.concatenate(
                    [jnp.where(targets[i, a] == window, solved[a], jnp.zeros_like(solved[a])) for i in range(k)], axis=1
                )
                for window in windows
            ],
            axis=0,
        )
        copies[a].wait()
        part = dot(lhs, blocks[a].reshape(k * width, wide))
        if a == 0:
            acc[...] = part
        elif a + 1 < leaves:
            acc[...] += part
        else:
            total = acc[...] + part
            keep_ref[...] = total[: 2 * nrhs].reshape(2, nrhs, wide)
            give_ref[...] = total[2 * nrhs :].astype(BF16).reshape(2, nrhs, wide)


def parent_forward_kernel(keep, came, rhs, lower, across, *rest):
    sums, half_ref = rest[:-1], rest[-1]
    _, core, parent = place()
    cut = lower.shape[2]
    update = keep[0] + came[0].astype(F32)
    for term in sums:
        update = update + term[...].astype(F32)
    combined = (rhs[parent].astype(F32) - update).astype(BF16)
    half_ref[:, columns(core, cut)] = dot(combined, lower[parent]).astype(BF16)
    half_ref[:, columns(1 - core, cut)] = dot(combined, across[0]).astype(BF16)


def through_upper(forward, of, source, depth, upper, across):
    rows = pl.ds(pl.multiple_of(source * depth, depth), depth)
    return dot(forward, upper[of, rows, :]), dot(forward, across[1 + of, rows, :])


def parent_early_kernel(mine, theirs, upper, across, part_ref):
    chip, core, parent = place()
    cut = upper.shape[2]
    for of, forward in ((parent, mine), (1 - parent, theirs)):
        here, there = through_upper(forward[...], of, chip, forward.shape[1], upper, across)
        part_ref[of, :, columns(core, cut)] = here
        part_ref[of, :, columns(1 - core, cut)] = there


def parent_backward_kernel(part, mine, theirs, upper, across, parent_ref, half_ref):
    chip, core, parent = place()
    cut = upper.shape[2]
    moved, _, depth = mine.shape
    for of, arrived in ((parent, mine), (1 - parent, theirs)):
        here, there = part[of, :, columns(core, cut)], part[of, :, columns(1 - core, cut)]
        for by in range(1, moved + 1):
            source = lax.rem(chip + moved + 1 - by, moved + 1)
            more_here, more_there = through_upper(arrived[by - 1], of, source, depth, upper, across)
            here, there = here + more_here, there + more_there
        parent_ref[of] = here
        half_ref[of, :, columns(core, cut)] = here.astype(BF16)
        half_ref[of, :, columns(1 - core, cut)] = there.astype(BF16)


def backward_kernel(targets, full, solved, mine, theirs, blocks, upper, *rest):
    halves, (leaf_ref, parent_ref, window) = rest[:-3], rest[-3:]
    parent_ref[...] = full[...]
    leaves, k, wide, width = blocks.shape
    chips = len(halves)
    depth = wide // chips
    chip, core, _ = place()
    for by, half in enumerate(halves):
        window[pl.ds(0, 2), :, columns(lax.rem(chip + chips - by, chips), depth)] = half[...]
    for by in range(0, chips, CORES):
        for arrived, lag in ((mine, core), (theirs, 1 - core)):
            at = columns(lax.rem(chip + chips - by - lag, chips), depth)
            window[pl.ds(2, 2), :, at] = arrived[by // CORES]
    listed = targets[...]
    couplings = [
        functools.reduce(jnp.add, [dot(window[listed[i, a]], blocks[a, i]) for i in range(k)]) for a in range(leaves)
    ]
    for a in range(leaves):
        reduced = (solved[a].astype(F32) - couplings[a]).astype(BF16)
        leaf_ref[a] = dot(reduced, upper[a])


def local(
    right_side, leaf_lower, leaf_upper, lower_blocks, upper_blocks, parent_rhs, parent_lower, parent_upper, targets
):
    rows, cols = lax.axis_size("row"), lax.axis_size("col")
    chips = cols // CORES
    go = functools.partial(send, rows=rows, cols=cols)
    leaves, k, width, wide = lower_blocks.shape
    nrhs = right_side.shape[1]
    cut = parent_lower.shape[2]
    depth = cut * CORES
    listed = targets.T

    solved, keep, give = pl.pallas_call(
        forward_kernel,
        in_specs=[HBM] * 4,
        out_specs=[VMEM] * 3,
        out_shape=[
            jax.ShapeDtypeStruct((leaves, nrhs, width), BF16),
            jax.ShapeDtypeStruct((2, nrhs, wide), F32),
            jax.ShapeDtypeStruct((2, nrhs, wide), BF16),
        ],
        scratch_shapes=[
            pltpu.SMEM(listed.shape, jnp.int32),
            pltpu.VMEM(right_side.shape, BF16),
            pltpu.VMEM(leaf_lower.shape, BF16),
            pltpu.VMEM(lower_blocks.shape, BF16),
            pltpu.VMEM((4 * nrhs, wide), F32),
            pltpu.SemaphoreType.DMA((3 + leaves,)),
        ],
        compiler_params=pltpu.CompilerParams(vmem_limit_bytes=24 << 20),
        cost_estimate=pl.CostEstimate(flops=1 << 29, bytes_accessed=5 << 20, transcendentals=0),
        name="forward",
    )(*in_hbm(listed, right_side, leaf_lower, lower_blocks))

    give, lower, upper = lax.optimization_barrier((give, parent_lower, parent_upper))
    came = go(give, by_row=0, target=along(0, 1))
    _, _, parent = place()
    across = jnp.concatenate([lax.dynamic_index_in_dim(lower, 1 - parent, 0), upper])
    came, across = lax.optimization_barrier((came, across))
    across = go(across, by_row=0, target=along(0, 1))
    own_sum = (keep[0] + came[0].astype(F32)).astype(BF16)
    next_sum = (keep[1] + came[1].astype(F32)).astype(BF16)
    sums = [go(next_sum, by_row=1, target=along(by, 1)) for by in reversed(range(chips))]
    sums += [go(own_sum, by_row=0, target=along(by)) for by in range(1, chips)]

    half = pl.pallas_call(
        parent_forward_kernel,
        in_specs=[VMEM] * (5 + len(sums)),
        out_specs=VMEM,
        out_shape=jax.ShapeDtypeStruct((nrhs, depth), BF16),
        compiler_params=pltpu.CompilerParams(vmem_limit_bytes=16 << 20),
        cost_estimate=pl.CostEstimate(flops=1 << 25, bytes_accessed=2 << 20, transcendentals=0),
        name="parent_forward",
    )(keep, came, parent_rhs, lower, across, *sums)
    mine = jnp.stack([go(half, by_row=0, target=along(by)) for by in range(1, chips)])
    other_half = go(half, by_row=0, target=along(0, 1))
    part = pl.pallas_call(
        parent_early_kernel,
        in_specs=[VMEM] * 4,
        out_specs=VMEM,
        out_shape=jax.ShapeDtypeStruct((2, nrhs, depth), F32),
        compiler_params=pltpu.CompilerParams(vmem_limit_bytes=16 << 20),
        cost_estimate=pl.CostEstimate(flops=1 << 26, bytes_accessed=2 << 20, transcendentals=0),
        name="parent_early",
    )(half, other_half, upper, across)
    theirs = go(mine, by_row=0, target=along(0, 1))

    full, half = pl.pallas_call(
        parent_backward_kernel,
        in_specs=[VMEM] * 5,
        out_specs=[VMEM, VMEM],
        out_shape=[jax.ShapeDtypeStruct((2, nrhs, cut), F32), jax.ShapeDtypeStruct((2, nrhs, depth), BF16)],
        compiler_params=pltpu.CompilerParams(vmem_limit_bytes=16 << 20),
        cost_estimate=pl.CostEstimate(flops=1 << 26, bytes_accessed=2 << 20, transcendentals=0),
        name="parent_backward",
    )(part, mine, theirs, upper, across)

    halves = [half] + [go(half, by_row=0, target=along(by, (by + 1) % CORES)) for by in range(1, chips)]
    mine = jnp.stack([go(half, by_row=-1, target=fan(by)) for by in range(0, chips, CORES)])
    theirs = go(mine, by_row=0, target=along(0, 1))

    return pl.pallas_call(
        backward_kernel,
        in_specs=[VMEM] * (7 + chips),
        out_specs=[VMEM, VMEM],
        out_shape=[jax.ShapeDtypeStruct((leaves, nrhs, width), F32), jax.ShapeDtypeStruct(full.shape, F32)],
        scratch_shapes=[pltpu.VMEM((4, nrhs, wide), BF16)],
        compiler_params=pltpu.CompilerParams(vmem_limit_bytes=24 << 20),
        cost_estimate=pl.CostEstimate(flops=1 << 28, bytes_accessed=5 << 20, transcendentals=0),
        name="backward",
    )(listed, full, solved, mine, theirs, upper_blocks, leaf_upper, *halves)


def solution(mesh):
    placed = (
        P(("row", "col"), None, None),
        P(("row", "col"), None, None),
        P(("row", "col"), None, None),
        P(("row", "col"), None, None, None),
        P(("row", "col"), None, None, None),
        P("row", None, None),
        P("row", None, "col"),
        P("row", None, "col"),
        P(("row", "col"), None),
    )
    return jax.shard_map(
        local,
        mesh=mesh,
        in_specs=placed,
        out_specs=(P(("row", "col"), None, None), P("row", None, "col")),
        check_vma=False,
    )
```

```python
import functools

import jax
import jax.numpy as jnp
from jax import lax
from jax.experimental import pallas as pl
from jax.experimental.pallas import tpu as pltpu
from jax.sharding import PartitionSpec as P

CORES = 2
F32 = jnp.float32
BF16 = jnp.bfloat16
VMEM = pl.BlockSpec(memory_space=pltpu.VMEM)
HBM = pl.BlockSpec(memory_space=pltpu.HBM)


def dot(a, b):
    return jnp.dot(a, b, preferred_element_type=F32)


def in_hbm(*arrays):
    return [pltpu.with_memory_space_constraint(array, pltpu.HBM) for array in arrays]


def place():
    here = lax.axis_index("col")
    chip, core = lax.div(here, CORES), lax.rem(here, CORES)
    return chip, core, lax.rem(chip + core, CORES)


def send(array, rows, cols, by_row, target):
    chips = cols // CORES
    pairs = []
    for row in range(rows):
        for col in range(cols):
            chip, core = target(col // CORES, col % CORES)
            pairs.append((row * cols + col, ((row + by_row) % rows) * cols + chip % chips * CORES + core))
    return lax.ppermute(array, ("row", "col"), pairs)


def along(by, other=0):
    return lambda chip, core: (chip + by, (core + by + other) % CORES)


def fan(by):
    return lambda chip, core: (chip + by + core, 1 - core)


def columns(index, size):
    return pl.ds(pl.multiple_of(index * size, size), size)


def forward_kernel(targets_hbm, rhs_hbm, lower_hbm, blocks_hbm, solved_ref, keep_ref, give_ref, targets, rhs, lower, blocks, acc, sems):
    leaves, k, width, wide = blocks.shape
    nrhs = rhs.shape[1]
    _, _, parent = place()
    first = [
        pltpu.make_async_copy(targets_hbm, targets, sems.at[0]),
        pltpu.make_async_copy(rhs_hbm, rhs, sems.at[1]),
        pltpu.make_async_copy(lower_hbm, lower, sems.at[2]),
    ]
    copies = [pltpu.make_async_copy(blocks_hbm.at[a], blocks.at[a], sems.at[3 + a]) for a in range(leaves)]
    for copy in first + copies:
        copy.start()
    windows = (parent, 3 - parent, 1 - parent, 2 + parent)
    for copy in first:
        copy.wait()
    solved = [dot(rhs[a], lower[a]).astype(BF16) for a in range(leaves)]
    for a in range(leaves):
        solved_ref[a] = solved[a]
    for a in range(leaves):
        lhs = jnp.concatenate(
            [
                jnp.concatenate(
                    [jnp.where(targets[i, a] == window, solved[a], jnp.zeros_like(solved[a])) for i in range(k)], axis=1
                )
                for window in windows
            ],
            axis=0,
        )
        copies[a].wait()
        part = dot(lhs, blocks[a].reshape(k * width, wide))
        if a == 0:
            acc[...] = part
        elif a + 1 < leaves:
            acc[...] += part
        else:
            total = acc[...] + part
            keep_ref[...] = total[: 2 * nrhs].reshape(2, nrhs, wide)
            give_ref[...] = total[2 * nrhs :].astype(BF16).reshape(2, nrhs, wide)


def parent_forward_kernel(keep, came, rhs, lower, across, *rest):
    sums, half_ref = rest[:-1], rest[-1]
    _, core, parent = place()
    cut = lower.shape[2]
    update = keep[0] + came[0].astype(F32)
    for term in sums:
        update = update + term[...].astype(F32)
    combined = (rhs[parent].astype(F32) - update).astype(BF16)
    half_ref[:, columns(core, cut)] = dot(combined, lower[parent]).astype(BF16)
    half_ref[:, columns(1 - core, cut)] = dot(combined, across[0]).astype(BF16)


def through_upper(forward, of, source, depth, upper, across):
    rows = pl.ds(pl.multiple_of(source * depth, depth), depth)
    return dot(forward, upper[of, rows, :]), dot(forward, across[1 + of, rows, :])


def parent_early_kernel(mine, theirs, upper, across, part_ref):
    chip, core, parent = place()
    cut = upper.shape[2]
    for of, forward in ((parent, mine), (1 - parent, theirs)):
        here, there = through_upper(forward[...], of, chip, forward.shape[1], upper, across)
        part_ref[of, :, columns(core, cut)] = here
        part_ref[of, :, columns(1 - core, cut)] = there


def parent_backward_kernel(part, mine, theirs, upper, across, parent_ref, half_ref):
    chip, core, parent = place()
    cut = upper.shape[2]
    moved, _, depth = mine.shape
    for of, arrived in ((parent, mine), (1 - parent, theirs)):
        here, there = part[of, :, columns(core, cut)], part[of, :, columns(1 - core, cut)]
        for by in range(1, moved + 1):
            source = lax.rem(chip + moved + 1 - by, moved + 1)
            more_here, more_there = through_upper(arrived[by - 1], of, source, depth, upper, across)
            here, there = here + more_here, there + more_there
        parent_ref[of] = here
        half_ref[of, :, columns(core, cut)] = here.astype(BF16)
        half_ref[of, :, columns(1 - core, cut)] = there.astype(BF16)


def backward_kernel(targets, full, solved, mine, theirs, blocks, upper, *rest):
    halves, (leaf_ref, parent_ref, window) = rest[:-3], rest[-3:]
    parent_ref[...] = full[...]
    leaves, k, wide, width = blocks.shape
    chips = len(halves)
    depth = wide // chips
    chip, core, _ = place()
    for by, half in enumerate(halves):
        window[pl.ds(0, 2), :, columns(lax.rem(chip + chips - by, chips), depth)] = half[...]
    for by in range(0, chips, CORES):
        for arrived, lag in ((mine, 1 - core), (theirs, core)):
            at = columns(lax.rem(chip + chips - by - lag, chips), depth)
            window[pl.ds(2, 2), :, at] = arrived[by // CORES]
    listed = targets[...]
    couplings = [
        functools.reduce(jnp.add, [dot(window[listed[i, a]], blocks[a, i]) for i in range(k)]) for a in range(leaves)
    ]
    for a in range(leaves):
        reduced = (solved[a].astype(F32) - couplings[a]).astype(BF16)
        leaf_ref[a] = dot(reduced, upper[a])


def local(
    right_side, leaf_lower, leaf_upper, lower_blocks, upper_blocks, parent_rhs, parent_lower, parent_upper, targets
):
    rows, cols = lax.axis_size("row"), lax.axis_size("col")
    chips = cols // CORES
    go = functools.partial(send, rows=rows, cols=cols)
    leaves, k, width, wide = lower_blocks.shape
    nrhs = right_side.shape[1]
    cut = parent_lower.shape[2]
    depth = cut * CORES
    listed = targets.T

    solved, keep, give = pl.pallas_call(
        forward_kernel,
        in_specs=[HBM] * 4,
        out_specs=[VMEM] * 3,
        out_shape=[
            jax.ShapeDtypeStruct((leaves, nrhs, width), BF16),
            jax.ShapeDtypeStruct((2, nrhs, wide), F32),
            jax.ShapeDtypeStruct((2, nrhs, wide), BF16),
        ],
        scratch_shapes=[
            pltpu.SMEM(listed.shape, jnp.int32),
            pltpu.VMEM(right_side.shape, BF16),
            pltpu.VMEM(leaf_lower.shape, BF16),
            pltpu.VMEM(lower_blocks.shape, BF16),
            pltpu.VMEM((4 * nrhs, wide), F32),
            pltpu.SemaphoreType.DMA((3 + leaves,)),
        ],
        compiler_params=pltpu.CompilerParams(vmem_limit_bytes=24 << 20),
        cost_estimate=pl.CostEstimate(flops=1 << 29, bytes_accessed=5 << 20, transcendentals=0),
        name="forward",
    )(*in_hbm(listed, right_side, leaf_lower, lower_blocks))

    give, lower, upper = lax.optimization_barrier((give, parent_lower, parent_upper))
    came = go(give, by_row=0, target=along(0, 1))
    _, _, parent = place()
    across = jnp.concatenate([lax.dynamic_index_in_dim(lower, 1 - parent, 0), upper])
    came, across = lax.optimization_barrier((came, across))
    across = go(across, by_row=0, target=along(0, 1))
    own_sum = (keep[0] + came[0].astype(F32)).astype(BF16)
    next_sum = (keep[1] + came[1].astype(F32)).astype(BF16)
    sums = [go(next_sum, by_row=1, target=along(by, 1)) for by in reversed(range(chips))]
    sums += [go(own_sum, by_row=0, target=along(by)) for by in range(1, chips)]

    half = pl.pallas_call(
        parent_forward_kernel,
        in_specs=[VMEM] * (5 + len(sums)),
        out_specs=VMEM,
        out_shape=jax.ShapeDtypeStruct((nrhs, depth), BF16),
        compiler_params=pltpu.CompilerParams(vmem_limit_bytes=16 << 20),
        cost_estimate=pl.CostEstimate(flops=1 << 25, bytes_accessed=2 << 20, transcendentals=0),
        name="parent_forward",
    )(keep, came, parent_rhs, lower, across, *sums)
    mine = jnp.stack([go(half, by_row=0, target=along(by)) for by in range(1, chips)])
    other_half = go(half, by_row=0, target=along(0, 1))
    part = pl.pallas_call(
        parent_early_kernel,
        in_specs=[VMEM] * 4,
        out_specs=VMEM,
        out_shape=jax.ShapeDtypeStruct((2, nrhs, depth), F32),
        compiler_params=pltpu.CompilerParams(vmem_limit_bytes=16 << 20),
        cost_estimate=pl.CostEstimate(flops=1 << 26, bytes_accessed=2 << 20, transcendentals=0),
        name="parent_early",
    )(half, other_half, upper, across)
    theirs = go(mine, by_row=0, target=along(0, 1))

    full, half = pl.pallas_call(
        parent_backward_kernel,
        in_specs=[VMEM] * 5,
        out_specs=[VMEM, VMEM],
        out_shape=[jax.ShapeDtypeStruct((2, nrhs, cut), F32), jax.ShapeDtypeStruct((2, nrhs, depth), BF16)],
        compiler_params=pltpu.CompilerParams(vmem_limit_bytes=16 << 20),
        cost_estimate=pl.CostEstimate(flops=1 << 26, bytes_accessed=2 << 20, transcendentals=0),
        name="parent_backward",
    )(part, mine, theirs, upper, across)

    halves = [half] + [go(half, by_row=0, target=along(by, (by + 1) % CORES)) for by in range(1, chips)]
    mine = jnp.stack([go(half, by_row=-1, target=fan(by)) for by in range(0, chips, CORES)])
    theirs = go(mine, by_row=0, target=along(0, 1))

    return pl.pallas_call(
        backward_kernel,
        in_specs=[VMEM] * (7 + chips),
        out_specs=[VMEM, VMEM],
        out_shape=[jax.ShapeDtypeStruct((leaves, nrhs, width), F32), jax.ShapeDtypeStruct(full.shape, F32)],
        scratch_shapes=[pltpu.VMEM((4, nrhs, wide), BF16)],
        compiler_params=pltpu.CompilerParams(vmem_limit_bytes=24 << 20),
        cost_estimate=pl.CostEstimate(flops=1 << 28, bytes_accessed=5 << 20, transcendentals=0),
        name="backward",
    )(listed, full, solved, mine, theirs, upper_blocks, leaf_upper, *halves)


def solution(mesh):
    placed = (
        P(("row", "col"), None, None),
        P(("row", "col"), None, None),
        P(("row", "col"), None, None),
        P(("row", "col"), None, None, None),
        P(("row", "col"), None, None, None),
        P("row", None, None),
        P("row", None, "col"),
        P("row", None, "col"),
        P(("row", "col"), None),
    )
    return jax.shard_map(
        local,
        mesh=mesh,
        in_specs=placed,
        out_specs=(P(("row", "col"), None, None), P("row", None, "col")),
        check_vma=False,
    )
```

```python
import functools

import jax
import jax.numpy as jnp
from jax import lax
from jax.experimental import pallas as pl
from jax.experimental.pallas import tpu as pltpu
from jax.sharding import PartitionSpec as P

CORES = 2
F32 = jnp.float32
BF16 = jnp.bfloat16
VMEM = pl.BlockSpec(memory_space=pltpu.VMEM)
HBM = pl.BlockSpec(memory_space=pltpu.HBM)


def dot(a, b):
    return jnp.dot(a, b, preferred_element_type=F32)


def in_hbm(*arrays):
    return [pltpu.with_memory_space_constraint(array, pltpu.HBM) for array in arrays]


def place():
    here = lax.axis_index("col")
    chip, core = lax.div(here, CORES), lax.rem(here, CORES)
    return chip, core, lax.rem(chip + core, CORES)


def send(array, rows, cols, by_row, target):
    chips = cols // CORES
    pairs = []
    for row in range(rows):
        for col in range(cols):
            chip, core = target(col // CORES, col % CORES)
            pairs.append((row * cols + col, ((row + by_row) % rows) * cols + chip % chips * CORES + core))
    return lax.ppermute(array, ("row", "col"), pairs)


def along(by, other=0):
    return lambda chip, core: (chip + by, (core + by + other) % CORES)


def fan(by):
    return lambda chip, core: (chip + by + core, 1 - core)


def columns(index, size):
    return pl.ds(pl.multiple_of(index * size, size), size)


def forward_kernel(targets_hbm, rhs_hbm, lower_hbm, blocks_hbm, solved_ref, keep_ref, give_ref, targets, rhs, lower, blocks, acc, sems):
    leaves, k, width, wide = blocks.shape
    nrhs = rhs.shape[1]
    _, _, parent = place()
    first = [
        pltpu.make_async_copy(targets_hbm, targets, sems.at[0]),
        pltpu.make_async_copy(rhs_hbm, rhs, sems.at[1]),
        pltpu.make_async_copy(lower_hbm, lower, sems.at[2]),
    ]
    copies = [pltpu.make_async_copy(blocks_hbm.at[a], blocks.at[a], sems.at[3 + a]) for a in range(leaves)]
    for copy in first + copies:
        copy.start()
    windows = (parent, 3 - parent, 1 - parent, 2 + parent)
    for copy in first:
        copy.wait()
    solved = [dot(rhs[a], lower[a]).astype(BF16) for a in range(leaves)]
    for a in range(leaves):
        solved_ref[a] = solved[a]
    for a in range(leaves):
        lhs = jnp.concatenate(
            [
                jnp.concatenate(
                    [jnp.where(targets[i, a] == window, solved[a], jnp.zeros_like(solved[a])) for i in range(k)], axis=1
                )
                for window in windows
            ],
            axis=0,
        )
        copies[a].wait()
        part = dot(lhs, blocks[a].reshape(k * width, wide))
        if a == 0:
            acc[...] = part
        elif a + 1 < leaves:
            acc[...] += part
        else:
            total = acc[...] + part
            keep_ref[...] = total[: 2 * nrhs].reshape(2, nrhs, wide)
            give_ref[...] = total[2 * nrhs :].astype(BF16).reshape(2, nrhs, wide)


def parent_forward_kernel(keep, came, rhs, lower, across, *rest):
    sums, half_ref = rest[:-1], rest[-1]
    _, core, parent = place()
    cut = lower.shape[2]
    update = keep[0] + came[0].astype(F32)
    for term in sums:
        update = update + term[...].astype(F32)
    combined = (rhs[parent].astype(F32) - update).astype(BF16)
    half_ref[:, columns(core, cut)] = dot(combined, lower[parent]).astype(BF16)
    half_ref[:, columns(1 - core, cut)] = dot(combined, across[0]).astype(BF16)


def through_upper(forward, of, source, depth, upper, across):
    rows = pl.ds(pl.multiple_of(source * depth, depth), depth)
    return dot(forward, upper[of, rows, :]), dot(forward, across[1 + of, rows, :])


def parent_early_kernel(mine, theirs, upper, across, part_ref):
    chip, core, parent = place()
    cut = upper.shape[2]
    for of, forward in ((parent, mine), (1 - parent, theirs)):
        here, there = through_upper(forward[...], of, chip, forward.shape[1], upper, across)
        part_ref[of, :, columns(core, cut)] = here
        part_ref[of, :, columns(1 - core, cut)] = there


def parent_backward_kernel(part, mine, theirs, upper, across, parent_ref, half_ref):
    chip, core, parent = place()
    cut = upper.shape[2]
    moved, _, depth = mine.shape
    for of, arrived in ((parent, mine), (1 - parent, theirs)):
        here, there = part[of, :, columns(core, cut)], part[of, :, columns(1 - core, cut)]
        for by in range(1, moved + 1):
            source = lax.rem(chip + moved + 1 - by, moved + 1)
            more_here, more_there = through_upper(arrived[by - 1], of, source, depth, upper, across)
            here, there = here + more_here, there + more_there
        parent_ref[of] = here
        half_ref[of, :, columns(core, cut)] = here.astype(BF16)
        half_ref[of, :, columns(1 - core, cut)] = there.astype(BF16)


def fill_window(window, halves, nexts, lag):
    chip, _, _ = place()
    chips, depth = len(halves), halves[0].shape[2]
    for by, half in enumerate(halves):
        window[pl.ds(0, 2), :, columns(lax.rem(chip + chips - by, chips), depth)] = half[...]
    parts = [columns(lax.rem(chip + chips - by - lag, chips), depth) for by in range(0, chips, CORES)]
    for i, at in enumerate(parts):
        window[pl.ds(2, 2), :, at] = nexts[i]
    return parts


def coupled(window, listed, blocks, a, parts):
    return functools.reduce(
        jnp.add, [dot(window[listed[i, a], :, at], blocks[a, i, at, :]) for i in range(blocks.shape[1]) for at in parts]
    )


def backward_first_kernel(targets, nexts, half, blocks, upper, part_ref, window):
    chip, core, _ = place()
    depth = half.shape[2]
    rows = columns(chip, depth)

    @pl.when(core == 1)
    def _():
        window[pl.ds(0, 2)] = half[...]
        window[pl.ds(2, 2)] = nexts[0]
        listed = targets[...]
        for a in range(blocks.shape[0]):
            part_ref[a] = functools.reduce(
                jnp.add, [dot(window[listed[i, a]], blocks[a, i, rows, :]) for i in range(blocks.shape[1])]
            )

    @pl.when(core == 0)
    def _():
        part_ref[...] = jnp.zeros_like(part_ref)


def backward_second_kernel(targets, nexts, blocks, first, *rest):
    halves, (part_ref, window) = rest[:-2], rest[-2:]
    _, core, _ = place()
    part_ref[...] = first[...]

    def add(parts):
        listed = targets[...]
        for a in range(blocks.shape[0]):
            part_ref[a] += coupled(window, listed, blocks, a, parts)

    chips = len(halves)
    if chips > CORES:
        add(fill_window(window, halves, nexts, 1 - core)[1:])

    @pl.when(core == 0)
    def _():
        add(fill_window(window, halves, nexts, 1 - core)[:1])


def backward_kernel(targets, full, solved, part, nexts, blocks, upper, *rest):
    halves, (leaf_ref, parent_ref, window) = rest[:-3], rest[-3:]
    _, core, _ = place()
    parent_ref[...] = full[...]
    parts = fill_window(window, halves, nexts, core)
    listed = targets[...]
    leaves = blocks.shape[0]
    couplings = [part[a] + coupled(window, listed, blocks, a, parts) for a in range(leaves)]
    for a in range(leaves):
        reduced = (solved[a].astype(F32) - couplings[a]).astype(BF16)
        leaf_ref[a] = dot(reduced, upper[a])


def local(
    right_side, leaf_lower, leaf_upper, lower_blocks, upper_blocks, parent_rhs, parent_lower, parent_upper, targets
):
    rows, cols = lax.axis_size("row"), lax.axis_size("col")
    chips = cols // CORES
    go = functools.partial(send, rows=rows, cols=cols)
    leaves, k, width, wide = lower_blocks.shape
    nrhs = right_side.shape[1]
    cut = parent_lower.shape[2]
    depth = cut * CORES
    listed = targets.T

    solved, keep, give = pl.pallas_call(
        forward_kernel,
        in_specs=[HBM] * 4,
        out_specs=[VMEM] * 3,
        out_shape=[
            jax.ShapeDtypeStruct((leaves, nrhs, width), BF16),
            jax.ShapeDtypeStruct((2, nrhs, wide), F32),
            jax.ShapeDtypeStruct((2, nrhs, wide), BF16),
        ],
        scratch_shapes=[
            pltpu.SMEM(listed.shape, jnp.int32),
            pltpu.VMEM(right_side.shape, BF16),
            pltpu.VMEM(leaf_lower.shape, BF16),
            pltpu.VMEM(lower_blocks.shape, BF16),
            pltpu.VMEM((4 * nrhs, wide), F32),
            pltpu.SemaphoreType.DMA((3 + leaves,)),
        ],
        compiler_params=pltpu.CompilerParams(vmem_limit_bytes=24 << 20),
        cost_estimate=pl.CostEstimate(flops=1 << 29, bytes_accessed=5 << 20, transcendentals=0),
        name="forward",
    )(*in_hbm(listed, right_side, leaf_lower, lower_blocks))

    give, lower, upper = lax.optimization_barrier((give, parent_lower, parent_upper))
    came = go(give, by_row=0, target=along(0, 1))
    _, _, parent = place()
    across = jnp.concatenate([lax.dynamic_index_in_dim(lower, 1 - parent, 0), upper])
    came, across = lax.optimization_barrier((came, across))
    across = go(across, by_row=0, target=along(0, 1))
    own_sum = (keep[0] + came[0].astype(F32)).astype(BF16)
    next_sum = (keep[1] + came[1].astype(F32)).astype(BF16)
    sums = [go(next_sum, by_row=1, target=along(by, 1)) for by in reversed(range(chips))]
    sums += [go(own_sum, by_row=0, target=along(by)) for by in range(1, chips)]

    half = pl.pallas_call(
        parent_forward_kernel,
        in_specs=[VMEM] * (5 + len(sums)),
        out_specs=VMEM,
        out_shape=jax.ShapeDtypeStruct((nrhs, depth), BF16),
        compiler_params=pltpu.CompilerParams(vmem_limit_bytes=16 << 20),
        cost_estimate=pl.CostEstimate(flops=1 << 25, bytes_accessed=2 << 20, transcendentals=0),
        name="parent_forward",
    )(keep, came, parent_rhs, lower, across, *sums)
    mine = jnp.stack([go(half, by_row=0, target=along(by)) for by in range(1, chips)])
    other_half = go(half, by_row=0, target=along(0, 1))
    part = pl.pallas_call(
        parent_early_kernel,
        in_specs=[VMEM] * 4,
        out_specs=VMEM,
        out_shape=jax.ShapeDtypeStruct((2, nrhs, depth), F32),
        compiler_params=pltpu.CompilerParams(vmem_limit_bytes=16 << 20),
        cost_estimate=pl.CostEstimate(flops=1 << 26, bytes_accessed=2 << 20, transcendentals=0),
        name="parent_early",
    )(half, other_half, upper, across)
    theirs = go(mine, by_row=0, target=along(0, 1))

    full, half = pl.pallas_call(
        parent_backward_kernel,
        in_specs=[VMEM] * 5,
        out_specs=[VMEM, VMEM],
        out_shape=[jax.ShapeDtypeStruct((2, nrhs, cut), F32), jax.ShapeDtypeStruct((2, nrhs, depth), BF16)],
        compiler_params=pltpu.CompilerParams(vmem_limit_bytes=16 << 20),
        cost_estimate=pl.CostEstimate(flops=1 << 26, bytes_accessed=2 << 20, transcendentals=0),
        name="parent_backward",
    )(part, mine, theirs, upper, across)

    halves = [half] + [go(half, by_row=0, target=along(by, (by + 1) % CORES)) for by in range(1, chips)]
    mine = jnp.stack([go(half, by_row=-1, target=fan(by)) for by in range(0, chips, CORES)])
    theirs = go(mine, by_row=0, target=along(0, 1))

    first = pl.pallas_call(
        backward_first_kernel,
        in_specs=[VMEM] * 5,
        out_specs=VMEM,
        out_shape=jax.ShapeDtypeStruct((leaves, nrhs, width), F32),
        scratch_shapes=[pltpu.VMEM((4, nrhs, depth), BF16)],
        compiler_params=pltpu.CompilerParams(vmem_limit_bytes=16 << 20),
        cost_estimate=pl.CostEstimate(flops=1 << 26, bytes_accessed=2 << 20, transcendentals=0),
        name="backward_first",
    )(listed, mine, half, upper_blocks, leaf_upper)
    part = pl.pallas_call(
        backward_second_kernel,
        in_specs=[VMEM] * (4 + chips),
        out_specs=VMEM,
        out_shape=jax.ShapeDtypeStruct((leaves, nrhs, width), F32),
        scratch_shapes=[pltpu.VMEM((4, nrhs, wide), BF16)],
        compiler_params=pltpu.CompilerParams(vmem_limit_bytes=16 << 20),
        cost_estimate=pl.CostEstimate(flops=1 << 26, bytes_accessed=2 << 20, transcendentals=0),
        name="backward_second",
    )(listed, mine, upper_blocks, first, *halves)

    return pl.pallas_call(
        backward_kernel,
        in_specs=[VMEM] * (7 + chips),
        out_specs=[VMEM, VMEM],
        out_shape=[
            jax.ShapeDtypeStruct((leaves, nrhs, width), F32),
            jax.ShapeDtypeStruct(full.shape, F32),
        ],
        scratch_shapes=[pltpu.VMEM((4, nrhs, wide), BF16)],
        compiler_params=pltpu.CompilerParams(vmem_limit_bytes=16 << 20),
        cost_estimate=pl.CostEstimate(flops=1 << 27, bytes_accessed=3 << 20, transcendentals=0),
        name="backward",
    )(listed, full, solved, part, theirs, upper_blocks, leaf_upper, *halves)


def solution(mesh):
    placed = (
        P(("row", "col"), None, None),
        P(("row", "col"), None, None),
        P(("row", "col"), None, None),
        P(("row", "col"), None, None, None),
        P(("row", "col"), None, None, None),
        P("row", None, None),
        P("row", None, "col"),
        P("row", None, "col"),
        P(("row", "col"), None),
    )
    return jax.shard_map(
        local,
        mesh=mesh,
        in_specs=placed,
        out_specs=(P(("row", "col"), None, None), P("row", None, "col")),
        check_vma=False,
    )
```

```python
import functools

import jax
import jax.numpy as jnp
from jax import lax
from jax.experimental import pallas as pl
from jax.experimental.pallas import tpu as pltpu
from jax.sharding import PartitionSpec as P

CORES = 2
F32 = jnp.float32
BF16 = jnp.bfloat16
VMEM = pl.BlockSpec(memory_space=pltpu.VMEM)
HBM = pl.BlockSpec(memory_space=pltpu.HBM)


def dot(a, b):
    return jnp.dot(a, b, preferred_element_type=F32)


def in_hbm(*arrays):
    return [pltpu.with_memory_space_constraint(array, pltpu.HBM) for array in arrays]


def place():
    here = lax.axis_index("col")
    chip, core = lax.div(here, CORES), lax.rem(here, CORES)
    return chip, core, lax.rem(chip + core, CORES)


def send(array, rows, cols, by_row, target):
    chips = cols // CORES
    pairs = []
    for row in range(rows):
        for col in range(cols):
            chip, core = target(col // CORES, col % CORES)
            pairs.append((row * cols + col, ((row + by_row) % rows) * cols + chip % chips * CORES + core))
    return lax.ppermute(array, ("row", "col"), pairs)


def along(by, other=0):
    return lambda chip, core: (chip + by, (core + by + other) % CORES)


def fan(by):
    return lambda chip, core: (chip + by + core, 1 - core)


def columns(index, size):
    return pl.ds(pl.multiple_of(index * size, size), size)


def forward_kernel(targets_hbm, rhs_hbm, lower_hbm, blocks_hbm, solved_ref, keep_ref, give_ref, targets, rhs, lower, blocks, acc, sems):
    leaves, k, width, wide = blocks.shape
    nrhs = rhs.shape[1]
    _, _, parent = place()
    first = [
        pltpu.make_async_copy(targets_hbm, targets, sems.at[0]),
        pltpu.make_async_copy(rhs_hbm, rhs, sems.at[1]),
        pltpu.make_async_copy(lower_hbm, lower, sems.at[2]),
    ]
    copies = [pltpu.make_async_copy(blocks_hbm.at[a], blocks.at[a], sems.at[3 + a]) for a in range(leaves)]
    for copy in first + copies:
        copy.start()
    windows = (parent, 3 - parent, 1 - parent, 2 + parent)
    for copy in first:
        copy.wait()
    solved = [dot(rhs[a], lower[a]).astype(BF16) for a in range(leaves)]
    for a in range(leaves):
        solved_ref[a] = solved[a]
    for a in range(leaves):
        lhs = jnp.concatenate(
            [
                jnp.concatenate(
                    [jnp.where(targets[i, a] == window, solved[a], jnp.zeros_like(solved[a])) for i in range(k)], axis=1
                )
                for window in windows
            ],
            axis=0,
        )
        copies[a].wait()
        part = dot(lhs, blocks[a].reshape(k * width, wide))
        if a == 0:
            acc[...] = part
        elif a + 1 < leaves:
            acc[...] += part
        else:
            total = acc[...] + part
            keep_ref[...] = total[: 2 * nrhs].reshape(2, nrhs, wide)
            give_ref[...] = total[2 * nrhs :].astype(BF16).reshape(2, nrhs, wide)


def parent_forward_kernel(keep, came, rhs, lower, across, *rest):
    sums, half_ref = rest[:-1], rest[-1]
    _, core, parent = place()
    cut = lower.shape[2]
    update = keep[0] + came[0].astype(F32)
    for term in sums:
        update = update + term[...].astype(F32)
    combined = (rhs[parent].astype(F32) - update).astype(BF16)
    half_ref[:, columns(core, cut)] = dot(combined, lower[parent]).astype(BF16)
    half_ref[:, columns(1 - core, cut)] = dot(combined, across[0]).astype(BF16)


def through_upper(forward, of, source, depth, upper, across):
    rows = pl.ds(pl.multiple_of(source * depth, depth), depth)
    return dot(forward, upper[of, rows, :]), dot(forward, across[1 + of, rows, :])


def parent_early_kernel(mine, theirs, upper, across, part_ref):
    chip, core, parent = place()
    cut = upper.shape[2]
    for of, forward in ((parent, mine), (1 - parent, theirs)):
        here, there = through_upper(forward[...], of, chip, forward.shape[1], upper, across)
        part_ref[of, :, columns(core, cut)] = here
        part_ref[of, :, columns(1 - core, cut)] = there


def parent_backward_kernel(part, mine, theirs, upper, across, parent_ref, half_ref):
    chip, core, parent = place()
    cut = upper.shape[2]
    moved, _, depth = mine.shape
    for of, arrived in ((parent, mine), (1 - parent, theirs)):
        here, there = part[of, :, columns(core, cut)], part[of, :, columns(1 - core, cut)]
        for by in range(1, moved + 1):
            source = lax.rem(chip + moved + 1 - by, moved + 1)
            more_here, more_there = through_upper(arrived[by - 1], of, source, depth, upper, across)
            here, there = here + more_here, there + more_there
        parent_ref[of] = here
        half_ref[of, :, columns(core, cut)] = here.astype(BF16)
        half_ref[of, :, columns(1 - core, cut)] = there.astype(BF16)


def fill_window(window, halves, nexts, lag):
    chip, _, _ = place()
    chips, depth = len(halves), halves[0].shape[2]
    for by, half in enumerate(halves):
        window[pl.ds(0, 2), :, columns(lax.rem(chip + chips - by, chips), depth)] = half[...]
    parts = [columns(lax.rem(chip + chips - by - lag, chips), depth) for by in range(0, chips, CORES)]
    for i, at in enumerate(parts):
        window[pl.ds(2, 2), :, at] = nexts[i]
    return parts


def coupled(window, listed, blocks, a, parts):
    return functools.reduce(
        jnp.add, [dot(window[listed[i, a], :, at], blocks[a, i, at, :]) for i in range(blocks.shape[1]) for at in parts]
    )


def backward_first_kernel(targets, nexts, half, blocks, upper, part_ref, window):
    chip, core, _ = place()
    depth = half.shape[2]
    rows = columns(chip, depth)

    @pl.when(core == 1)
    def _():
        window[pl.ds(0, 2)] = half[...]
        window[pl.ds(2, 2)] = nexts[0]
        listed = targets[...]
        for a in range(blocks.shape[0]):
            part_ref[a] = functools.reduce(
                jnp.add, [dot(window[listed[i, a]], blocks[a, i, rows, :]) for i in range(blocks.shape[1])]
            )

    @pl.when(core == 0)
    def _():
        part_ref[...] = jnp.zeros_like(part_ref)


def backward_second_kernel(targets, nexts, blocks, first, *rest):
    halves, (part_ref, window) = rest[:-2], rest[-2:]
    _, core, _ = place()
    part_ref[...] = first[...]

    def add(parts):
        listed = targets[...]
        for a in range(blocks.shape[0]):
            part_ref[a] += coupled(window, listed, blocks, a, parts)

    chips = len(halves)
    if chips > CORES:
        add(fill_window(window, halves, nexts, 1 - core)[1:])

    @pl.when(core == 0)
    def _():
        add(fill_window(window, halves, nexts, 1 - core)[:1])


def backward_kernel(targets, full, solved, part, nexts, blocks, upper, *rest):
    halves, (leaf_ref, parent_ref, window) = rest[:-3], rest[-3:]
    _, core, _ = place()
    parent_ref[...] = full[...]
    parts = fill_window(window, halves, nexts, core)
    listed = targets[...]
    leaves = blocks.shape[0]
    couplings = [part[a] + coupled(window, listed, blocks, a, parts) for a in range(leaves)]
    for a in range(leaves):
        reduced = (solved[a].astype(F32) - couplings[a]).astype(BF16)
        leaf_ref[a] = dot(reduced, upper[a])


def local(
    right_side, leaf_lower, leaf_upper, lower_blocks, upper_blocks, parent_rhs, parent_lower, parent_upper, targets
):
    rows, cols = lax.axis_size("row"), lax.axis_size("col")
    chips = cols // CORES
    go = functools.partial(send, rows=rows, cols=cols)
    leaves, k, width, wide = lower_blocks.shape
    nrhs = right_side.shape[1]
    cut = parent_lower.shape[2]
    depth = cut * CORES
    listed = targets.T

    solved, keep, give = pl.pallas_call(
        forward_kernel,
        in_specs=[HBM] * 4,
        out_specs=[VMEM] * 3,
        out_shape=[
            jax.ShapeDtypeStruct((leaves, nrhs, width), BF16),
            jax.ShapeDtypeStruct((2, nrhs, wide), F32),
            jax.ShapeDtypeStruct((2, nrhs, wide), BF16),
        ],
        scratch_shapes=[
            pltpu.SMEM(listed.shape, jnp.int32),
            pltpu.VMEM(right_side.shape, BF16),
            pltpu.VMEM(leaf_lower.shape, BF16),
            pltpu.VMEM(lower_blocks.shape, BF16),
            pltpu.VMEM((4 * nrhs, wide), F32),
            pltpu.SemaphoreType.DMA((3 + leaves,)),
        ],
        compiler_params=pltpu.CompilerParams(vmem_limit_bytes=24 << 20),
        cost_estimate=pl.CostEstimate(flops=1 << 29, bytes_accessed=5 << 20, transcendentals=0),
        name="forward",
    )(*in_hbm(listed, right_side, leaf_lower, lower_blocks))

    give, lower, upper = lax.optimization_barrier((give, parent_lower, parent_upper))
    came = go(give, by_row=0, target=along(0, 1))
    _, _, parent = place()
    across = jnp.concatenate([lax.dynamic_index_in_dim(lower, 1 - parent, 0), upper])
    came, across = lax.optimization_barrier((came, across))
    across = go(across, by_row=0, target=along(0, 1))
    own_sum = (keep[0] + came[0].astype(F32)).astype(BF16)
    next_sum = (keep[1] + came[1].astype(F32)).astype(BF16)
    sums = [go(next_sum, by_row=1, target=along(by, 1)) for by in reversed(range(1, chips))]
    sums += [go(own_sum, by_row=0, target=along(by)) for by in range(1, chips)]
    sums += [go(next_sum, by_row=1, target=along(0, 1))]

    half = pl.pallas_call(
        parent_forward_kernel,
        in_specs=[VMEM] * (5 + len(sums)),
        out_specs=VMEM,
        out_shape=jax.ShapeDtypeStruct((nrhs, depth), BF16),
        compiler_params=pltpu.CompilerParams(vmem_limit_bytes=16 << 20),
        cost_estimate=pl.CostEstimate(flops=1 << 25, bytes_accessed=2 << 20, transcendentals=0),
        name="parent_forward",
    )(keep, came, parent_rhs, lower, across, *sums)
    mine = jnp.stack([go(half, by_row=0, target=along(by)) for by in range(1, chips)])
    other_half = go(half, by_row=0, target=along(0, 1))
    part = pl.pallas_call(
        parent_early_kernel,
        in_specs=[VMEM] * 4,
        out_specs=VMEM,
        out_shape=jax.ShapeDtypeStruct((2, nrhs, depth), F32),
        compiler_params=pltpu.CompilerParams(vmem_limit_bytes=16 << 20),
        cost_estimate=pl.CostEstimate(flops=1 << 26, bytes_accessed=2 << 20, transcendentals=0),
        name="parent_early",
    )(half, other_half, upper, across)
    theirs = go(mine, by_row=0, target=along(0, 1))

    full, half = pl.pallas_call(
        parent_backward_kernel,
        in_specs=[VMEM] * 5,
        out_specs=[VMEM, VMEM],
        out_shape=[jax.ShapeDtypeStruct((2, nrhs, cut), F32), jax.ShapeDtypeStruct((2, nrhs, depth), BF16)],
        compiler_params=pltpu.CompilerParams(vmem_limit_bytes=16 << 20),
        cost_estimate=pl.CostEstimate(flops=1 << 26, bytes_accessed=2 << 20, transcendentals=0),
        name="parent_backward",
    )(part, mine, theirs, upper, across)

    halves = [half] + [go(half, by_row=0, target=along(by, (by + 1) % CORES)) for by in range(1, chips)]
    mine = jnp.stack([go(half, by_row=-1, target=fan(by)) for by in range(0, chips, CORES)])
    theirs = go(mine, by_row=0, target=along(0, 1))

    first = pl.pallas_call(
        backward_first_kernel,
        in_specs=[VMEM] * 5,
        out_specs=VMEM,
        out_shape=jax.ShapeDtypeStruct((leaves, nrhs, width), F32),
        scratch_shapes=[pltpu.VMEM((4, nrhs, depth), BF16)],
        compiler_params=pltpu.CompilerParams(vmem_limit_bytes=16 << 20),
        cost_estimate=pl.CostEstimate(flops=1 << 26, bytes_accessed=2 << 20, transcendentals=0),
        name="backward_first",
    )(listed, mine, half, upper_blocks, leaf_upper)
    part = pl.pallas_call(
        backward_second_kernel,
        in_specs=[VMEM] * (4 + chips),
        out_specs=VMEM,
        out_shape=jax.ShapeDtypeStruct((leaves, nrhs, width), F32),
        scratch_shapes=[pltpu.VMEM((4, nrhs, wide), BF16)],
        compiler_params=pltpu.CompilerParams(vmem_limit_bytes=16 << 20),
        cost_estimate=pl.CostEstimate(flops=1 << 26, bytes_accessed=2 << 20, transcendentals=0),
        name="backward_second",
    )(listed, mine, upper_blocks, first, *halves)

    return pl.pallas_call(
        backward_kernel,
        in_specs=[VMEM] * (7 + chips),
        out_specs=[VMEM, VMEM],
        out_shape=[
            jax.ShapeDtypeStruct((leaves, nrhs, width), F32),
            jax.ShapeDtypeStruct(full.shape, F32),
        ],
        scratch_shapes=[pltpu.VMEM((4, nrhs, wide), BF16)],
        compiler_params=pltpu.CompilerParams(vmem_limit_bytes=16 << 20),
        cost_estimate=pl.CostEstimate(flops=1 << 27, bytes_accessed=3 << 20, transcendentals=0),
        name="backward",
    )(listed, full, solved, part, theirs, upper_blocks, leaf_upper, *halves)


def solution(mesh):
    placed = (
        P(("row", "col"), None, None),
        P(("row", "col"), None, None),
        P(("row", "col"), None, None),
        P(("row", "col"), None, None, None),
        P(("row", "col"), None, None, None),
        P("row", None, None),
        P("row", None, "col"),
        P("row", None, "col"),
        P(("row", "col"), None),
    )
    return jax.shard_map(
        local,
        mesh=mesh,
        in_specs=placed,
        out_specs=(P(("row", "col"), None, None), P("row", None, "col")),
        check_vma=False,
    )
```

```python
import functools

import jax
import jax.numpy as jnp
from jax import lax
from jax.experimental import pallas as pl
from jax.experimental.pallas import tpu as pltpu
from jax.sharding import PartitionSpec as P

CORES = 2
F32 = jnp.float32
BF16 = jnp.bfloat16
VMEM = pl.BlockSpec(memory_space=pltpu.VMEM)
HBM = pl.BlockSpec(memory_space=pltpu.HBM)


def dot(a, b):
    return jnp.dot(a, b, preferred_element_type=F32)


def in_hbm(*arrays):
    return [pltpu.with_memory_space_constraint(array, pltpu.HBM) for array in arrays]


def place():
    here = lax.axis_index("col")
    chip, core = lax.div(here, CORES), lax.rem(here, CORES)
    return chip, core, lax.rem(chip + core, CORES)


def send(array, rows, cols, by_row, target):
    chips = cols // CORES
    pairs = []
    for row in range(rows):
        for col in range(cols):
            chip, core = target(col // CORES, col % CORES)
            pairs.append((row * cols + col, ((row + by_row) % rows) * cols + chip % chips * CORES + core))
    return lax.ppermute(array, ("row", "col"), pairs)


def along(by, other=0):
    return lambda chip, core: (chip + by, (core + by + other) % CORES)


def fan(by):
    return lambda chip, core: (chip + by + core, 1 - core)


def columns(index, size):
    return pl.ds(pl.multiple_of(index * size, size), size)


def forward_kernel(targets_hbm, rhs_hbm, lower_hbm, blocks_hbm, solved_ref, keep_ref, give_ref, targets, rhs, lower, blocks, acc, sems):
    leaves, k, width, wide = blocks.shape
    nrhs = rhs.shape[1]
    _, _, parent = place()
    first = [
        pltpu.make_async_copy(targets_hbm, targets, sems.at[0]),
        pltpu.make_async_copy(rhs_hbm, rhs, sems.at[1]),
        pltpu.make_async_copy(lower_hbm, lower, sems.at[2]),
    ]
    copies = [pltpu.make_async_copy(blocks_hbm.at[a], blocks.at[a], sems.at[3 + a]) for a in range(leaves)]
    for copy in first + copies:
        copy.start()
    windows = (parent, 3 - parent, 1 - parent, 2 + parent)
    for copy in first:
        copy.wait()
    solved = [dot(rhs[a], lower[a]).astype(BF16) for a in range(leaves)]
    for a in range(leaves):
        solved_ref[a] = solved[a]
    for a in range(leaves):
        lhs = jnp.concatenate(
            [
                jnp.concatenate(
                    [jnp.where(targets[i, a] == window, solved[a], jnp.zeros_like(solved[a])) for i in range(k)], axis=1
                )
                for window in windows
            ],
            axis=0,
        )
        copies[a].wait()
        part = dot(lhs, blocks[a].reshape(k * width, wide))
        if a == 0:
            acc[...] = part
        elif a + 1 < leaves:
            acc[...] += part
        else:
            total = acc[...] + part
            keep_ref[...] = total[: 2 * nrhs].reshape(2, nrhs, wide)
            give_ref[...] = total[2 * nrhs :].astype(BF16).reshape(2, nrhs, wide)


def parent_forward_kernel(keep, came, rhs, lower, across, *rest):
    sums, half_ref = rest[:-1], rest[-1]
    _, core, parent = place()
    cut = lower.shape[2]
    update = keep[0] + came[0].astype(F32)
    for term in sums:
        update = update + term[...].astype(F32)
    combined = (rhs[parent].astype(F32) - update).astype(BF16)
    half_ref[:, columns(core, cut)] = dot(combined, lower[parent]).astype(BF16)
    half_ref[:, columns(1 - core, cut)] = dot(combined, across[0]).astype(BF16)


def through_upper(forward, of, source, depth, upper, across):
    rows = pl.ds(pl.multiple_of(source * depth, depth), depth)
    return dot(forward, upper[of, rows, :]), dot(forward, across[1 + of, rows, :])


def parent_early_kernel(mine, theirs, upper, across, part_ref):
    chip, core, parent = place()
    cut = upper.shape[2]
    for of, forward in ((parent, mine), (1 - parent, theirs)):
        here, there = through_upper(forward[...], of, chip, forward.shape[1], upper, across)
        part_ref[of, :, columns(core, cut)] = here
        part_ref[of, :, columns(1 - core, cut)] = there


def parent_backward_kernel(part, mine, theirs, upper, across, parent_ref, half_ref):
    chip, core, parent = place()
    cut = upper.shape[2]
    moved, _, depth = mine.shape
    for of, arrived in ((parent, mine), (1 - parent, theirs)):
        here, there = part[of, :, columns(core, cut)], part[of, :, columns(1 - core, cut)]
        for by in range(1, moved + 1):
            source = lax.rem(chip + moved + 1 - by, moved + 1)
            more_here, more_there = through_upper(arrived[by - 1], of, source, depth, upper, across)
            here, there = here + more_here, there + more_there
        parent_ref[of] = here
        half_ref[of, :, columns(core, cut)] = here.astype(BF16)
        half_ref[of, :, columns(1 - core, cut)] = there.astype(BF16)


def fill_window(window, halves, nexts, lag):
    chip, _, _ = place()
    chips, depth = len(halves), halves[0].shape[2]
    parts = [columns(lax.rem(chip + chips - by - lag, chips), depth) for by in range(0, chips, CORES)]
    for i, at in enumerate(parts):
        window[pl.ds(0, 2), :, at] = jnp.where(lag == 0, halves[CORES * i][...], halves[CORES * i + 1][...])
        window[pl.ds(2, 2), :, at] = nexts[i]
    return parts


def coupled(window, listed, blocks, a, parts):
    return functools.reduce(
        jnp.add, [dot(window[listed[i, a], :, at], blocks[a, i, at, :]) for i in range(blocks.shape[1]) for at in parts]
    )


def backward_first_kernel(targets, nexts, half, blocks, upper, part_ref, window):
    chip, core, _ = place()
    depth = half.shape[2]
    rows = columns(chip, depth)

    @pl.when(core == 1)
    def _():
        window[pl.ds(0, 2)] = half[...]
        window[pl.ds(2, 2)] = nexts[0]
        listed = targets[...]
        for a in range(blocks.shape[0]):
            part_ref[a] = functools.reduce(
                jnp.add, [dot(window[listed[i, a]], blocks[a, i, rows, :]) for i in range(blocks.shape[1])]
            )

    @pl.when(core == 0)
    def _():
        part_ref[...] = jnp.zeros_like(part_ref)


def backward_second_kernel(targets, nexts, blocks, first, *rest):
    halves, (part_ref, window) = rest[:-2], rest[-2:]
    _, core, _ = place()
    part_ref[...] = first[...]

    def add(parts):
        listed = targets[...]
        for a in range(blocks.shape[0]):
            part_ref[a] += coupled(window, listed, blocks, a, parts)

    chips = len(halves)
    if chips > CORES:
        add(fill_window(window, halves, nexts, 1 - core)[1:])

    @pl.when(core == 0)
    def _():
        add(fill_window(window, halves, nexts, 1 - core)[:1])


def backward_kernel(targets, full, solved, part, nexts, blocks, upper, *rest):
    halves, (leaf_ref, parent_ref, window) = rest[:-3], rest[-3:]
    _, core, _ = place()
    parent_ref[...] = full[...]
    parts = fill_window(window, halves, nexts, core)
    listed = targets[...]
    leaves = blocks.shape[0]
    couplings = [part[a] + coupled(window, listed, blocks, a, parts) for a in range(leaves)]
    for a in range(leaves):
        reduced = (solved[a].astype(F32) - couplings[a]).astype(BF16)
        leaf_ref[a] = dot(reduced, upper[a])


def local(
    right_side, leaf_lower, leaf_upper, lower_blocks, upper_blocks, parent_rhs, parent_lower, parent_upper, targets
):
    rows, cols = lax.axis_size("row"), lax.axis_size("col")
    chips = cols // CORES
    go = functools.partial(send, rows=rows, cols=cols)
    leaves, k, width, wide = lower_blocks.shape
    nrhs = right_side.shape[1]
    cut = parent_lower.shape[2]
    depth = cut * CORES
    listed = targets.T

    solved, keep, give = pl.pallas_call(
        forward_kernel,
        in_specs=[HBM] * 4,
        out_specs=[VMEM] * 3,
        out_shape=[
            jax.ShapeDtypeStruct((leaves, nrhs, width), BF16),
            jax.ShapeDtypeStruct((2, nrhs, wide), F32),
            jax.ShapeDtypeStruct((2, nrhs, wide), BF16),
        ],
        scratch_shapes=[
            pltpu.SMEM(listed.shape, jnp.int32),
            pltpu.VMEM(right_side.shape, BF16),
            pltpu.VMEM(leaf_lower.shape, BF16),
            pltpu.VMEM(lower_blocks.shape, BF16),
            pltpu.VMEM((4 * nrhs, wide), F32),
            pltpu.SemaphoreType.DMA((3 + leaves,)),
        ],
        compiler_params=pltpu.CompilerParams(vmem_limit_bytes=24 << 20),
        cost_estimate=pl.CostEstimate(flops=1 << 29, bytes_accessed=5 << 20, transcendentals=0),
        name="forward",
    )(*in_hbm(listed, right_side, leaf_lower, lower_blocks))

    give, lower, upper = lax.optimization_barrier((give, parent_lower, parent_upper))
    came = go(give, by_row=0, target=along(0, 1))
    _, _, parent = place()
    across = jnp.concatenate([lax.dynamic_index_in_dim(lower, 1 - parent, 0), upper])
    came, across = lax.optimization_barrier((came, across))
    across = go(across, by_row=0, target=along(0, 1))
    own_sum = (keep[0] + came[0].astype(F32)).astype(BF16)
    next_sum = (keep[1] + came[1].astype(F32)).astype(BF16)
    sums = [go(next_sum, by_row=1, target=along(by, 1)) for by in reversed(range(1, chips))]
    sums += [go(own_sum, by_row=0, target=along(by)) for by in range(1, chips)]
    sums += [go(next_sum, by_row=1, target=along(0, 1))]

    half = pl.pallas_call(
        parent_forward_kernel,
        in_specs=[VMEM] * (5 + len(sums)),
        out_specs=VMEM,
        out_shape=jax.ShapeDtypeStruct((nrhs, depth), BF16),
        compiler_params=pltpu.CompilerParams(vmem_limit_bytes=16 << 20),
        cost_estimate=pl.CostEstimate(flops=1 << 25, bytes_accessed=2 << 20, transcendentals=0),
        name="parent_forward",
    )(keep, came, parent_rhs, lower, across, *sums)
    mine = jnp.stack([go(half, by_row=0, target=along(by)) for by in range(1, chips)])
    other_half = go(half, by_row=0, target=along(0, 1))
    part = pl.pallas_call(
        parent_early_kernel,
        in_specs=[VMEM] * 4,
        out_specs=VMEM,
        out_shape=jax.ShapeDtypeStruct((2, nrhs, depth), F32),
        compiler_params=pltpu.CompilerParams(vmem_limit_bytes=16 << 20),
        cost_estimate=pl.CostEstimate(flops=1 << 26, bytes_accessed=2 << 20, transcendentals=0),
        name="parent_early",
    )(half, other_half, upper, across)
    theirs = go(mine, by_row=0, target=along(0, 1))

    full, half = pl.pallas_call(
        parent_backward_kernel,
        in_specs=[VMEM] * 5,
        out_specs=[VMEM, VMEM],
        out_shape=[jax.ShapeDtypeStruct((2, nrhs, cut), F32), jax.ShapeDtypeStruct((2, nrhs, depth), BF16)],
        compiler_params=pltpu.CompilerParams(vmem_limit_bytes=16 << 20),
        cost_estimate=pl.CostEstimate(flops=1 << 26, bytes_accessed=2 << 20, transcendentals=0),
        name="parent_backward",
    )(part, mine, theirs, upper, across)

    halves = [half] + [go(half, by_row=0, target=along(by, (by + 1) % CORES)) for by in range(1, chips)]
    mine = jnp.stack([go(half, by_row=-1, target=fan(by)) for by in range(0, chips, CORES)])
    theirs = go(mine, by_row=0, target=along(0, 1))

    first = pl.pallas_call(
        backward_first_kernel,
        in_specs=[VMEM] * 5,
        out_specs=VMEM,
        out_shape=jax.ShapeDtypeStruct((leaves, nrhs, width), F32),
        scratch_shapes=[pltpu.VMEM((4, nrhs, depth), BF16)],
        compiler_params=pltpu.CompilerParams(vmem_limit_bytes=16 << 20),
        cost_estimate=pl.CostEstimate(flops=1 << 26, bytes_accessed=2 << 20, transcendentals=0),
        name="backward_first",
    )(listed, mine, half, upper_blocks, leaf_upper)
    part = pl.pallas_call(
        backward_second_kernel,
        in_specs=[VMEM] * (4 + chips),
        out_specs=VMEM,
        out_shape=jax.ShapeDtypeStruct((leaves, nrhs, width), F32),
        scratch_shapes=[pltpu.VMEM((4, nrhs, wide), BF16)],
        compiler_params=pltpu.CompilerParams(vmem_limit_bytes=16 << 20),
        cost_estimate=pl.CostEstimate(flops=1 << 26, bytes_accessed=2 << 20, transcendentals=0),
        name="backward_second",
    )(listed, mine, upper_blocks, first, *halves)

    return pl.pallas_call(
        backward_kernel,
        in_specs=[VMEM] * (7 + chips),
        out_specs=[VMEM, VMEM],
        out_shape=[
            jax.ShapeDtypeStruct((leaves, nrhs, width), F32),
            jax.ShapeDtypeStruct(full.shape, F32),
        ],
        scratch_shapes=[pltpu.VMEM((4, nrhs, wide), BF16)],
        compiler_params=pltpu.CompilerParams(vmem_limit_bytes=16 << 20),
        cost_estimate=pl.CostEstimate(flops=1 << 27, bytes_accessed=3 << 20, transcendentals=0),
        name="backward",
    )(listed, full, solved, part, theirs, upper_blocks, leaf_upper, *halves)


def solution(mesh):
    placed = (
        P(("row", "col"), None, None),
        P(("row", "col"), None, None),
        P(("row", "col"), None, None),
        P(("row", "col"), None, None, None),
        P(("row", "col"), None, None, None),
        P("row", None, None),
        P("row", None, "col"),
        P("row", None, "col"),
        P(("row", "col"), None),
    )
    return jax.shard_map(
        local,
        mesh=mesh,
        in_specs=placed,
        out_specs=(P(("row", "col"), None, None), P("row", None, "col")),
        check_vma=False,
    )
```

```python
import functools

import jax
import jax.numpy as jnp
from jax import lax
from jax.experimental import pallas as pl
from jax.experimental.pallas import tpu as pltpu
from jax.sharding import PartitionSpec as P

CORES = 2
F32 = jnp.float32
BF16 = jnp.bfloat16
VMEM = pl.BlockSpec(memory_space=pltpu.VMEM)
HBM = pl.BlockSpec(memory_space=pltpu.HBM)


def dot(a, b):
    return jnp.dot(a, b, preferred_element_type=F32)


def in_hbm(*arrays):
    return [pltpu.with_memory_space_constraint(array, pltpu.HBM) for array in arrays]


def place():
    here = lax.axis_index("col")
    chip, core = lax.div(here, CORES), lax.rem(here, CORES)
    return chip, core, lax.rem(chip + core, CORES)


def send(array, rows, cols, by_row, target):
    chips = cols // CORES
    pairs = []
    for row in range(rows):
        for col in range(cols):
            chip, core = target(col // CORES, col % CORES)
            pairs.append((row * cols + col, ((row + by_row) % rows) * cols + chip % chips * CORES + core))
    return lax.ppermute(array, ("row", "col"), pairs)


def along(by, other=0):
    return lambda chip, core: (chip + by, (core + by + other) % CORES)


def fan(by):
    return lambda chip, core: (chip + by + core, 1 - core)


def columns(index, size):
    return pl.ds(pl.multiple_of(index * size, size), size)


def forward_kernel(targets_hbm, rhs_hbm, lower_hbm, blocks_hbm, solved_ref, keep_ref, give_ref, targets, rhs, lower, blocks, acc, sems):
    leaves, k, width, wide = blocks.shape
    nrhs = rhs.shape[1]
    _, _, parent = place()
    first = [
        pltpu.make_async_copy(targets_hbm, targets, sems.at[0]),
        pltpu.make_async_copy(rhs_hbm, rhs, sems.at[1]),
        pltpu.make_async_copy(lower_hbm, lower, sems.at[2]),
    ]
    copies = [pltpu.make_async_copy(blocks_hbm.at[a], blocks.at[a], sems.at[3 + a]) for a in range(leaves)]
    for copy in first + copies:
        copy.start()
    windows = (parent, 3 - parent, 1 - parent, 2 + parent)
    for copy in first:
        copy.wait()
    solved = [dot(rhs[a], lower[a]).astype(BF16) for a in range(leaves)]
    for a in range(leaves):
        solved_ref[a] = solved[a]
    for a in range(leaves):
        lhs = jnp.concatenate(
            [
                jnp.concatenate(
                    [jnp.where(targets[i, a] == window, solved[a], jnp.zeros_like(solved[a])) for i in range(k)], axis=1
                )
                for window in windows
            ],
            axis=0,
        )
        copies[a].wait()
        part = dot(lhs, blocks[a].reshape(k * width, wide))
        if a == 0:
            acc[...] = part
        elif a + 1 < leaves:
            acc[...] += part
        else:
            total = acc[...] + part
            keep_ref[...] = total[: 2 * nrhs].reshape(2, nrhs, wide)
            give_ref[...] = total[2 * nrhs :].astype(BF16).reshape(2, nrhs, wide)


def parent_forward_kernel(keep, came, rhs, lower, across, *rest):
    sums, half_ref = rest[:-1], rest[-1]
    _, core, parent = place()
    cut = lower.shape[2]
    update = keep[0] + came[0].astype(F32)
    for term in sums:
        update = update + term[...].astype(F32)
    combined = (rhs[parent].astype(F32) - update).astype(BF16)
    half_ref[:, columns(core, cut)] = dot(combined, lower[parent]).astype(BF16)
    half_ref[:, columns(1 - core, cut)] = dot(combined, across[0]).astype(BF16)


def through_upper(forward, of, source, depth, upper, across):
    rows = pl.ds(pl.multiple_of(source * depth, depth), depth)
    return dot(forward, upper[of, rows, :]), dot(forward, across[1 + of, rows, :])


def parent_early_kernel(mine, theirs, upper, across, leaf_upper, part_ref):
    chip, core, parent = place()
    cut = upper.shape[2]
    for of, forward in ((parent, mine), (1 - parent, theirs)):
        here, there = through_upper(forward[...], of, chip, forward.shape[1], upper, across)
        part_ref[of, :, columns(core, cut)] = here
        part_ref[of, :, columns(1 - core, cut)] = there


def parent_backward_kernel(part, mine, theirs, upper, across, parent_ref, half_ref):
    chip, core, parent = place()
    cut = upper.shape[2]
    moved, _, depth = mine.shape
    for of, arrived in ((parent, mine), (1 - parent, theirs)):
        here, there = part[of, :, columns(core, cut)], part[of, :, columns(1 - core, cut)]
        for by in range(1, moved + 1):
            source = lax.rem(chip + moved + 1 - by, moved + 1)
            more_here, more_there = through_upper(arrived[by - 1], of, source, depth, upper, across)
            here, there = here + more_here, there + more_there
        parent_ref[of] = here
        half_ref[of, :, columns(core, cut)] = here.astype(BF16)
        half_ref[of, :, columns(1 - core, cut)] = there.astype(BF16)


def fill_window(window, halves, nexts, lag):
    chip, _, _ = place()
    chips, depth = len(halves), halves[0].shape[2]
    for by, half in enumerate(halves):
        window[pl.ds(0, 2), :, columns(lax.rem(chip + chips - by, chips), depth)] = half[...]
    parts = [columns(lax.rem(chip + chips - by - lag, chips), depth) for by in range(0, chips, CORES)]
    for i, at in enumerate(parts):
        window[pl.ds(2, 2), :, at] = nexts[i]
    return parts


def coupled(window, listed, blocks, a, parts):
    return functools.reduce(
        jnp.add, [dot(window[listed[i, a], :, at], blocks[a, i, at, :]) for i in range(blocks.shape[1]) for at in parts]
    )


def backward_first_kernel(targets, nexts, half, blocks, part_ref, window):
    chip, core, _ = place()
    depth = half.shape[2]
    rows = columns(chip, depth)

    @pl.when(core == 1)
    def _():
        window[pl.ds(0, 2)] = half[...]
        window[pl.ds(2, 2)] = nexts[0]
        listed = targets[...]
        for a in range(blocks.shape[0]):
            part_ref[a] = functools.reduce(
                jnp.add, [dot(window[listed[i, a]], blocks[a, i, rows, :]) for i in range(blocks.shape[1])]
            )

    @pl.when(core == 0)
    def _():
        part_ref[...] = jnp.zeros_like(part_ref)


def backward_second_kernel(targets, nexts, blocks, first, *rest):
    halves, (part_ref, window) = rest[:-2], rest[-2:]
    _, core, _ = place()
    part_ref[...] = first[...]

    def add(parts):
        listed = targets[...]
        for a in range(blocks.shape[0]):
            part_ref[a] += coupled(window, listed, blocks, a, parts)

    chips = len(halves)
    if chips > CORES:
        add(fill_window(window, halves, nexts, 1 - core)[1:])

    @pl.when(core == 0)
    def _():
        add(fill_window(window, halves, nexts, 1 - core)[:1])


def backward_kernel(targets, full, solved, part, nexts, blocks, upper, *rest):
    halves, (leaf_ref, parent_ref, window) = rest[:-3], rest[-3:]
    _, core, _ = place()
    parent_ref[...] = full[...]
    parts = fill_window(window, halves, nexts, core)
    listed = targets[...]
    leaves = blocks.shape[0]
    couplings = [part[a] + coupled(window, listed, blocks, a, parts) for a in range(leaves)]
    for a in range(leaves):
        reduced = (solved[a].astype(F32) - couplings[a]).astype(BF16)
        leaf_ref[a] = dot(reduced, upper[a])


def local(
    right_side, leaf_lower, leaf_upper, lower_blocks, upper_blocks, parent_rhs, parent_lower, parent_upper, targets
):
    rows, cols = lax.axis_size("row"), lax.axis_size("col")
    chips = cols // CORES
    go = functools.partial(send, rows=rows, cols=cols)
    leaves, k, width, wide = lower_blocks.shape
    nrhs = right_side.shape[1]
    cut = parent_lower.shape[2]
    depth = cut * CORES
    listed = targets.T

    solved, keep, give = pl.pallas_call(
        forward_kernel,
        in_specs=[HBM] * 4,
        out_specs=[VMEM] * 3,
        out_shape=[
            jax.ShapeDtypeStruct((leaves, nrhs, width), BF16),
            jax.ShapeDtypeStruct((2, nrhs, wide), F32),
            jax.ShapeDtypeStruct((2, nrhs, wide), BF16),
        ],
        scratch_shapes=[
            pltpu.SMEM(listed.shape, jnp.int32),
            pltpu.VMEM(right_side.shape, BF16),
            pltpu.VMEM(leaf_lower.shape, BF16),
            pltpu.VMEM(lower_blocks.shape, BF16),
            pltpu.VMEM((4 * nrhs, wide), F32),
            pltpu.SemaphoreType.DMA((3 + leaves,)),
        ],
        compiler_params=pltpu.CompilerParams(vmem_limit_bytes=24 << 20),
        cost_estimate=pl.CostEstimate(flops=1 << 29, bytes_accessed=5 << 20, transcendentals=0),
        name="forward",
    )(*in_hbm(listed, right_side, leaf_lower, lower_blocks))

    give, lower, upper = lax.optimization_barrier((give, parent_lower, parent_upper))
    came = go(give, by_row=0, target=along(0, 1))
    _, _, parent = place()
    across = jnp.concatenate([lax.dynamic_index_in_dim(lower, 1 - parent, 0), upper])
    came, across = lax.optimization_barrier((came, across))
    across = go(across, by_row=0, target=along(0, 1))
    own_sum = (keep[0] + came[0].astype(F32)).astype(BF16)
    next_sum = (keep[1] + came[1].astype(F32)).astype(BF16)
    sums = [go(next_sum, by_row=1, target=along(by, 1)) for by in reversed(range(1, chips))]
    sums += [go(own_sum, by_row=0, target=along(by)) for by in range(1, chips)]
    sums += [go(next_sum, by_row=1, target=along(0, 1))]

    half = pl.pallas_call(
        parent_forward_kernel,
        in_specs=[VMEM] * (5 + len(sums)),
        out_specs=VMEM,
        out_shape=jax.ShapeDtypeStruct((nrhs, depth), BF16),
        compiler_params=pltpu.CompilerParams(vmem_limit_bytes=16 << 20),
        cost_estimate=pl.CostEstimate(flops=1 << 25, bytes_accessed=2 << 20, transcendentals=0),
        name="parent_forward",
    )(keep, came, parent_rhs, lower, across, *sums)
    mine = jnp.stack([go(half, by_row=0, target=along(by)) for by in range(1, chips)])
    other_half = go(half, by_row=0, target=along(0, 1))
    part = pl.pallas_call(
        parent_early_kernel,
        in_specs=[VMEM] * 5,
        out_specs=VMEM,
        out_shape=jax.ShapeDtypeStruct((2, nrhs, depth), F32),
        compiler_params=pltpu.CompilerParams(vmem_limit_bytes=16 << 20),
        cost_estimate=pl.CostEstimate(flops=1 << 26, bytes_accessed=2 << 20, transcendentals=0),
        name="parent_early",
    )(half, other_half, upper, across, leaf_upper)
    theirs = go(mine, by_row=0, target=along(0, 1))

    full, half = pl.pallas_call(
        parent_backward_kernel,
        in_specs=[VMEM] * 5,
        out_specs=[VMEM, VMEM],
        out_shape=[jax.ShapeDtypeStruct((2, nrhs, cut), F32), jax.ShapeDtypeStruct((2, nrhs, depth), BF16)],
        compiler_params=pltpu.CompilerParams(vmem_limit_bytes=16 << 20),
        cost_estimate=pl.CostEstimate(flops=1 << 26, bytes_accessed=2 << 20, transcendentals=0),
        name="parent_backward",
    )(part, mine, theirs, upper, across)

    halves = [half] + [go(half, by_row=0, target=along(by, (by + 1) % CORES)) for by in range(1, chips)]
    mine = jnp.stack([go(half, by_row=-1, target=fan(by)) for by in range(0, chips, CORES)])
    theirs = go(mine, by_row=0, target=along(0, 1))

    first = pl.pallas_call(
        backward_first_kernel,
        in_specs=[VMEM] * 4,
        out_specs=VMEM,
        out_shape=jax.ShapeDtypeStruct((leaves, nrhs, width), F32),
        scratch_shapes=[pltpu.VMEM((4, nrhs, depth), BF16)],
        compiler_params=pltpu.CompilerParams(vmem_limit_bytes=16 << 20),
        cost_estimate=pl.CostEstimate(flops=1 << 26, bytes_accessed=2 << 20, transcendentals=0),
        name="backward_first",
    )(listed, mine, half, upper_blocks)
    part = pl.pallas_call(
        backward_second_kernel,
        in_specs=[VMEM] * (4 + chips),
        out_specs=VMEM,
        out_shape=jax.ShapeDtypeStruct((leaves, nrhs, width), F32),
        scratch_shapes=[pltpu.VMEM((4, nrhs, wide), BF16)],
        compiler_params=pltpu.CompilerParams(vmem_limit_bytes=16 << 20),
        cost_estimate=pl.CostEstimate(flops=1 << 26, bytes_accessed=2 << 20, transcendentals=0),
        name="backward_second",
    )(listed, mine, upper_blocks, first, *halves)

    return pl.pallas_call(
        backward_kernel,
        in_specs=[VMEM] * (7 + chips),
        out_specs=[VMEM, VMEM],
        out_shape=[
            jax.ShapeDtypeStruct((leaves, nrhs, width), F32),
            jax.ShapeDtypeStruct(full.shape, F32),
        ],
        scratch_shapes=[pltpu.VMEM((4, nrhs, wide), BF16)],
        compiler_params=pltpu.CompilerParams(vmem_limit_bytes=16 << 20),
        cost_estimate=pl.CostEstimate(flops=1 << 27, bytes_accessed=3 << 20, transcendentals=0),
        name="backward",
    )(listed, full, solved, part, theirs, upper_blocks, leaf_upper, *halves)


def solution(mesh):
    placed = (
        P(("row", "col"), None, None),
        P(("row", "col"), None, None),
        P(("row", "col"), None, None),
        P(("row", "col"), None, None, None),
        P(("row", "col"), None, None, None),
        P("row", None, None),
        P("row", None, "col"),
        P("row", None, "col"),
        P(("row", "col"), None),
    )
    return jax.shard_map(
        local,
        mesh=mesh,
        in_specs=placed,
        out_specs=(P(("row", "col"), None, None), P("row", None, "col")),
        check_vma=False,
    )
```
